256 devices in a mesh: pipe: 32 (over y, z), dp: 8 (over x, core).
Axes of the slice: x: 4, y: 4, z: 8, core: 2. Of those that a mesh axis runs over, the one named last changes fastest.
Arguments:
- act_in: bfloat16 [8, 32, 128, 8192], P('dp', 'pipe'), may hold values from -6 to 6
- stash_a: bfloat16 [8, 32, 128, 8192], P('dp', 'pipe'), may hold values from -6 to 6
- grad_in: bfloat16 [8, 32, 128, 8192], P('dp', 'pipe'), may hold values from -6 to 6
- text_emb: bfloat16 [8, 128, 8192], P('dp', None, 'pipe'), may hold values from -6 to 6
- enc_query: bfloat16 [8, 128, 3200], P('dp', 'pipe'), may hold values from -32 to 32
- enc_key: bfloat16 [8, 2048, 3200], P('dp', 'pipe'), may hold values from -32 to 32
- enc_value: bfloat16 [8, 2048, 3200], P('dp', 'pipe'), may hold values from -6 to 6
- tok_count: int32 [8, 32], P('dp', 'pipe'), may hold values from 1 to 4, as said below
- tok_offset: int32 [8, 32], P('dp', 'pipe'), may hold values from 0 to 124, as said below
- merge_gain: float32 [3200], replicated, may hold values from 0.1 to 1.9
- w_merge: bfloat16 [3200, 128], P(None, 'dp'), may hold values from -0.109375 to 0.109375
- w_vision: bfloat16 [128, 8192], P(None, 'pipe'), may hold values from -0.5 to 0.5
- norm_gain: float32 [32, 8192], P('pipe'), may hold values from 0.1 to 1.9
- w_down: bfloat16 [32, 8192, 128], P('pipe', 'dp'), may hold values from -0.0625 to 0.0625
- w_up: bfloat16 [32, 128, 8192], P('pipe', None, 'dp'), may hold values from -0.5 to 0.5
Outputs:
- fwd_out: bfloat16 [8, 32, 128, 8192], P('dp', 'pipe')
- bwd_out: bfloat16 [8, 32, 128, 8192], P('dp', 'pipe')
- grad_down: float32 [32, 8192, 128], P('pipe', 'dp')
- grad_up: float32 [32, 128, 8192], P('pipe', None, 'dp')
The draws below stay inside these ranges and needn't reach their ends.
Inputs may be any that keep to these rules, and one draw needn't show every extreme that they name: `tok_count`: in every replica some section has exactly 4 image tokens. Section p's tokens occupy positions tok_offset to tok_offset + tok_count - 1; these ranges lie within the sequence, are disjoint and rise with p.
All inputs are finite; a program needn't handle non-finite values.
Results may differ from the reference program's by a relative error of at most 0.017.
Values may be sent and summed in bfloat16 or wider, within the bound.
A program may use at most 128 MiB of HBM per device.

```python
import jax
import jax.numpy as jnp
from jax import lax

D = 8192
R = 128
HEADS = 25
HEAD_DIM = 128
IMG = 64
S = 128
TMAX = 4
N_PIPE = 32
N_DP = 8


def section_layout(key):
    key_count, key_chosen, key_spacing = jax.random.split(key, 3)
    counts = jax.random.randint(key_count, (N_DP, N_PIPE), 1, TMAX + 1)
    chosen = jax.random.randint(key_chosen, (N_DP, 1), 0, N_PIPE)
    section_ids = jnp.arange(N_PIPE)[None, :]
    counts = jnp.where(section_ids == chosen, TMAX, counts)
    spacing = jax.random.randint(key_spacing, (N_DP, N_PIPE), 0, TMAX + 1) % (TMAX - counts + 1)
    spacing = jnp.where((section_ids == 0) | (section_ids == N_PIPE - 1), 0, spacing)
    offsets = section_ids * TMAX + spacing
    return (counts.astype(jnp.int32), offsets.astype(jnp.int32))


def draw_tok_count(key, part):
    layout = section_layout(key)
    return layout[0]


def draw_tok_offset(key, part):
    layout = section_layout(key)
    return layout[1]


def draw_enc_query(key, part):
    key = jax.random.fold_in(key, 1)
    width = HEADS * HEAD_DIM
    shape = (N_DP, N_PIPE * TMAX, width)
    return jnp.clip(jax.random.normal(key, shape, jnp.float32), -6.0, 6.0).astype(jnp.bfloat16)


def draw_enc_key(key, part):
    key = jax.random.fold_in(key, 2)
    shape = (N_DP, N_PIPE * IMG, HEADS * HEAD_DIM)
    noise = jax.random.normal(key, shape, jnp.float32)
    return jnp.clip(noise, -6.0, 6.0).astype(jnp.bfloat16)


def level_of(stream_key, dims, shards, low, largest):
    level = 1.0
    for position, shards_of in shards:
        steps = jax.random.uniform(jax.random.fold_in(jax.random.fold_in(stream_key, 6), position), (shards_of,), jnp.float32, low / len(shards), largest / len(shards))
        level = level * jnp.repeat(jnp.exp(steps), dims[position] // shards_of).reshape((-1,) + (1,) * (len(dims) - 1 - position))
    return level


def centred(rng, shape, deviation, bound, cuts=(), held_as=jnp.bfloat16):
    entries = jax.random.normal(rng, shape, jnp.float32) * deviation
    if len(cuts) > 0:
        entries = level_of(rng, shape, cuts, -0.22, 0.18) * entries
    return jnp.clip(entries, min=-bound, max=bound).astype(held_as)


def setup_inputs(seed: int = 0) -> dict:
    key_of = jax.random.split(jax.random.key(seed), 16)
    act_in = centred(key_of[0], (N_DP, N_PIPE, S, D), 1.0, 6.0, ((0, 8), (1, 32)))
    stash_a = centred(key_of[1], (N_DP, N_PIPE, S, D), 1.0, 6.0, ((0, 8), (1, 32)))
    grad_in = centred(key_of[2], (N_DP, N_PIPE, S, D), 1.0, 6.0, ((0, 8), (1, 32)))
    text_emb = centred(key_of[3], (N_DP, S, D), 1.0, 6.0, ((0, 8), (2, 32)))
    enc_query = draw_enc_query(jax.random.fold_in(key_of[15], 71), 0)
    enc_key = draw_enc_key(jax.random.fold_in(key_of[15], 71), 0)
    enc_value = centred(key_of[6], (N_DP, N_PIPE * IMG, HEADS * HEAD_DIM), 1.0, 6.0, ((0, 8), (1, 32)))
    tok_count = draw_tok_count(jax.random.fold_in(key_of[15], 71), 0)
    tok_offset = draw_tok_offset(jax.random.fold_in(key_of[15], 71), 0)
    merge_gain = jnp.clip(1.0 + 0.18 * jax.random.normal(key_of[9], (HEADS * HEAD_DIM,), jnp.float32), 0.1, 1.9)
    w_merge = centred(key_of[10], (HEADS * HEAD_DIM, R), (HEADS * HEAD_DIM) ** -0.5, 0.109375, ((1, 8),))
    w_vision = centred(key_of[11], (R, D), R ** -0.5, 0.5, ((1, 32),))
    norm_gain = jnp.clip(1.0 + 0.18 * jax.random.normal(key_of[12], (N_PIPE, D), jnp.float32), 0.1, 1.9)
    w_down = centred(key_of[13], (N_PIPE, D, R), D ** -0.5, 0.0625, ((0, 32), (1, 8)))
    w_up = centred(key_of[14], (N_PIPE, R, D), R ** -0.5, 0.5, ((0, 32), (2, 8)))
    return dict(act_in=act_in, stash_a=stash_a, grad_in=grad_in, text_emb=text_emb, enc_query=enc_query, enc_key=enc_key, enc_value=enc_value, tok_count=tok_count, tok_offset=tok_offset, merge_gain=merge_gain, w_merge=w_merge, w_vision=w_vision, norm_gain=norm_gain, w_down=w_down, w_up=w_up)


EPS = 1e-06

def swish(inner):
    return inner * jax.nn.sigmoid(inner)

def adapter_forward(x, gain, w_down, w_up):
    x32 = x.astype(jnp.float32)
    scale = lax.rsqrt(lax.optimization_barrier(jnp.mean(x32 * x32, -1, keepdims=True)) + EPS)
    normed = (x32 * scale * gain).astype(jnp.bfloat16)
    hidden = swish(jnp.dot(normed, w_down, preferred_element_type=jnp.float32)).astype(jnp.bfloat16)
    return (x32 + jnp.dot(hidden, w_up, preferred_element_type=jnp.float32)).astype(jnp.bfloat16)

def adapter_backward(x, grad_out, gain, w_down, w_up):
    x32 = x.astype(jnp.float32)
    scale = lax.rsqrt(lax.optimization_barrier(jnp.mean(x32 * x32, -1, keepdims=True)) + EPS)
    unit = x32 * scale
    normed = (unit * gain).astype(jnp.bfloat16)
    inner = jnp.dot(normed, w_down, preferred_element_type=jnp.float32)
    sig = jax.nn.sigmoid(inner)
    hidden = (inner * sig).astype(jnp.bfloat16)
    back_h = jnp.einsum('sd,rd->sr', grad_out.astype(jnp.float32), w_up.astype(jnp.float32))
    back_u = (back_h * sig * (1.0 + inner * (1.0 - sig))).astype(jnp.bfloat16)
    back_n = jnp.einsum('sr,dr->sd', back_u.astype(jnp.float32), w_down.astype(jnp.float32)) * gain
    back_x = scale * (back_n - unit * lax.optimization_barrier(jnp.mean(back_n * unit, -1, keepdims=True)))
    grad_x = (grad_out.astype(jnp.float32) + back_x).astype(jnp.bfloat16)
    down_term = jnp.einsum('sd,sr->dr', normed.astype(jnp.float32), back_u.astype(jnp.float32))
    up_term = jnp.einsum('sr,sd->rd', hidden.astype(jnp.float32), grad_out.astype(jnp.float32))
    return (grad_x, down_term, up_term)

def encode_section(query, keys, values):
    q3 = query.astype(jnp.float32).reshape(query.shape[0], HEADS, HEAD_DIM)
    k3 = keys.astype(jnp.float32).reshape(keys.shape[0], HEADS, HEAD_DIM)
    v3 = values.astype(jnp.float32).reshape(values.shape[0], HEADS, HEAD_DIM)
    scores = jnp.einsum('qhd,khd->hqk', q3, k3) * HEAD_DIM ** (-0.5)
    top = lax.optimization_barrier(jnp.max(scores, -1, keepdims=True))
    weights = jnp.exp(scores - top)
    probs = (weights / lax.optimization_barrier(jnp.sum(weights, -1, keepdims=True))).astype(jnp.bfloat16)
    attended = jnp.einsum('hqk,khd->qhd', probs.astype(jnp.float32), v3)
    return attended.reshape(query.shape[0], HEADS * HEAD_DIM).astype(jnp.bfloat16)

def merge_tokens(rows, gain, w_merge):
    x32 = rows.astype(jnp.float32)
    scale = lax.rsqrt(lax.optimization_barrier(jnp.mean(x32 * x32, -1, keepdims=True)) + EPS)
    normed = (x32 * scale * gain).astype(jnp.bfloat16)
    return jax.nn.gelu(jnp.dot(normed, w_merge, preferred_element_type=jnp.float32)).astype(jnp.bfloat16)

def place_rows(counts, offsets, seq_len, slots):
    slot_ids = jnp.arange(slots, dtype=jnp.int32)
    target = (offsets[:, None] + slot_ids[None, :]).reshape(-1)
    live = (slot_ids[None, :] < counts[:, None]).reshape(-1)
    return (jnp.arange(seq_len, dtype=jnp.int32)[:, None] == target[None, :]) & live[None, :]

def compose(vision, marked, text, w_vision):
    mapped = jnp.dot(vision, w_vision, preferred_element_type=jnp.float32)
    return jnp.where(marked[:, None], mapped, text.astype(jnp.float32)).astype(jnp.bfloat16)

def reference(act_in, stash_a, grad_in, text_emb, enc_query, enc_key, enc_value, tok_count, tok_offset, merge_gain, w_merge, w_vision, norm_gain, w_down, w_up):
    forward_all = jax.vmap(adapter_forward)
    backward_all = jax.vmap(adapter_backward)
    encode_all = jax.vmap(encode_section)
    total_down = jnp.zeros(w_down.shape, jnp.float32)
    total_up = jnp.zeros(w_up.shape, jnp.float32)
    fwd_list = []
    bwd_list = []
    for replica in range(N_DP):
        query = enc_query[replica].reshape(N_PIPE, TMAX, -1)
        keys = enc_key[replica].reshape(N_PIPE, IMG, -1)
        values = enc_value[replica].reshape(N_PIPE, IMG, -1)
        attended = encode_all(query, keys, values)
        tokens = merge_tokens(attended.reshape(N_PIPE * TMAX, -1), merge_gain, w_merge)
        placed = place_rows(tok_count[replica], tok_offset[replica], S, TMAX)
        vision = jnp.dot(placed.astype(jnp.bfloat16), tokens, preferred_element_type=jnp.float32).astype(jnp.bfloat16)
        marked = jnp.any(placed, 1)
        fresh = compose(vision, marked, text_emb[replica], w_vision)
        first = act_in[replica]
        out0 = forward_all(first, norm_gain, w_down, w_up)
        incoming = jnp.concatenate([fresh[None], out0[:-1]], 0)
        out1 = forward_all(incoming, norm_gain, w_down, w_up)
        final_out = adapter_forward(stash_a[replica, -1], norm_gain[-1], w_down[-1], w_up[-1])
        grad_first = jnp.concatenate([grad_in[replica, :-1], final_out[None]], 0)
        back0, down0, up0 = backward_all(stash_a[replica], grad_first, norm_gain, w_down, w_up)
        grad_second = jnp.concatenate([back0[1:], out0[-1:]], 0)
        back1, down1, up1 = backward_all(first, grad_second, norm_gain, w_down, w_up)
        total_down = total_down + down0 + down1
        total_up = total_up + up0 + up1
        fwd_list.append(out1)
        bwd_list.append(back1)
    return (jnp.stack(fwd_list, 0), jnp.stack(bwd_list, 0), total_down, total_up)
```

```python
import functools

import jax
import jax.numpy as jnp
from jax import lax
from jax.experimental import pallas as pl
from jax.experimental.pallas import tpu as pltpu
from jax.sharding import PartitionSpec as P

HEAD_DIM = 128
EPS = 1e-06
RING = 4
Z = 8
TOK = 16
MESH = pl.DeviceIdType.MESH
BF, F32 = jnp.bfloat16, jnp.float32


def mm(a, b):
    return jnp.dot(a, b, preferred_element_type=F32)


def mm_nt(a, b):
    return lax.dot_general(a, b, (((1,), (1,)), ((), ())), preferred_element_type=F32)


def mm_tn(a, b):
    return lax.dot_general(a, b, (((0,), (0,)), ((), ())), preferred_element_type=F32)


def swish(inner):
    return inner * jax.nn.sigmoid(inner)


def pick(k, values):
    out = jnp.int32(values[-1])
    for i in range(len(values) - 2, -1, -1):
        out = jnp.where(k == i, jnp.int32(values[i]), out)
    return out


def rcopy(src, dst, send_sem, recv_sem, device):
    return pltpu.make_async_remote_copy(
        src_ref=src,
        dst_ref=dst,
        send_sem=send_sem,
        recv_sem=recv_sem,
        device_id=device,
        device_id_type=MESH,
    )


FWD = (0, 3, 1, 2)
BWD = (2, 1, 3, 0)


def kernel(
    n_pipe,
    act_h, st_h, gin_h, text_h, wv_h, q_ref, ek_h, ev_h, cnt_ref, off_ref, mg_ref, wm_h, gain_ref, wd_h, wu_h,
    fwd_h, bwd_h, gd_h, gu_h,
    X, G, N, wd, wu, xin, O0, B0, nall, but, upf, ups, upr, uxs, uxr, dps, dpr, dxs, dxr, accu, accd,
    wm, ek, ev, text, wv, scr, att, tk, fb, fra, sc, inner, sig, hid, hidt, bh, bu, ic, ss, hid2, gdo,
    ld, ags, agr, aus, aur, wms, wmr, zfs, zfr, zbs, zbr, nas, nar, bus, bur,
    ups_s, ups_r, uxs_s, uxs_r, dps_s, dps_r, dxs_s, dxs_r, tzs, tzr, tys, tyr, fzs, fzr, fys, fyr, outs,
):
    nq, s2, db = X.shape
    s = s2 // 2
    r = wu.shape[1]
    dp_cols = fb.shape[1]
    per = db // dp_cols
    n_y = n_pipe // Z
    width = nq * db
    heads = att.shape[1] // HEAD_DIM

    p, d = lax.axis_index("pipe"), lax.axis_index("dp")
    y, z = p // Z, p % Z
    x, c = d // 2, d % 2
    last = p == n_pipe - 1
    xr, xl, xo = (x + 1) % RING, (x + 3) % RING, (x + 2) % RING

    def at(chip, core):
        return chip * 2 + core

    right, left, other, mate = (p, at(xr, c)), (p, at(xl, c)), (p, at(xo, c)), (p, at(x, 1 - c))

    def cols(ref, q):
        return ref.at[:, pl.ds(pl.multiple_of(q * db, 128), db)]

    def load(i, src, dst):
        return pltpu.make_async_copy(src, dst, ld.at[i])

    small = [
        lambda: load(0, wd_h, wd.at[d]),
        lambda: load(1, wu_h, wu.at[d]),
        lambda: load(2, wm_h, wm.at[d]),
        lambda: load(3, ek_h, ek),
        lambda: load(4, ev_h, ev),
        lambda: load(5, text_h, text),
        lambda: load(6, wv_h, wv),
    ]

    def big(q):
        return (
            load(8 + q, cols(act_h, q), X.at[q, pl.ds(0, s)]),
            load(8 + nq + q, cols(st_h, q), X.at[q, pl.ds(s, s)]),
            load(8 + 2 * nq + q, cols(gin_h, q), G.at[q, pl.ds(s, s)]),
        )

    for copy in small:
        copy().start()

    def start_big(q, carry):
        for copy in big(q):
            copy.start()
        return carry

    lax.fori_loop(0, nq, start_big, 0)

    barrier = pltpu.get_barrier_semaphore()

    def greet(device):
        pl.semaphore_signal(barrier, inc=1, device_id=device, device_id_type=MESH)

    for i in range(1, nq):
        greet((p, (d + i) % nq))
    for i in range(1, Z):
        greet((y * Z + (z + i) % Z, d))
    for i in range(1, n_y):
        greet((((y + i) % n_y) * Z + z, d))
    up_wrap = (z == Z - 1) & (y < n_y - 1)
    down_wrap = (z == 0) & (y > 0)

    @pl.when(up_wrap)
    def _():
        greet((p + 1, d))

    @pl.when(down_wrap)
    def _():
        greet((p - 1, d))

    extra = jnp.where(up_wrap | down_wrap, 1, 0)
    pl.semaphore_wait(barrier, nq - 1 + Z - 1 + n_y - 1 + extra)

    class Gather:
        def __init__(self, buf, send, recv):
            self.buf, self.send, self.recv = buf, send, recv
            self.half = buf.shape[1] // 2

        def copy(self, i):
            lo, hi = pl.ds(0, self.half), pl.ds(self.half, self.half)
            ref, device = (
                lambda: (self.buf.at[d], right),
                lambda: (self.buf.at[d], left),
                lambda: (self.buf.at[at(xl, c), lo], right),
                lambda: (self.buf.at[at(xr, c), hi], left),
                lambda: (self.buf.at[d], mate),
                lambda: (self.buf.at[at(xl, c)], mate),
                lambda: (self.buf.at[at(xr, c)], mate),
                lambda: (self.buf.at[at(xo, c)], mate),
            )[i]()
            return rcopy(ref, ref, self.send.at[i], self.recv.at[i], device)

        def arrival(self, i):
            lo, hi = pl.ds(0, self.half), pl.ds(self.half, self.half)
            ref = (
                lambda: self.buf.at[at(xl, c)],
                lambda: self.buf.at[at(xr, c)],
                lambda: self.buf.at[at(xo, c), lo],
                lambda: self.buf.at[at(xo, c), hi],
                lambda: self.buf.at[at(x, 1 - c)],
                lambda: self.buf.at[at(xl, 1 - c)],
                lambda: self.buf.at[at(xr, 1 - c)],
                lambda: self.buf.at[at(xo, 1 - c)],
            )[i]()
            return rcopy(ref, ref, self.send.at[i], self.recv.at[i], mate)

        def go(self, *which):
            for i in which:
                self.copy(i).start()

        def wait(self, *which):
            for i in which:
                self.arrival(i).wait_recv()

        def drain(self):
            for i in range(8):
                self.copy(i).wait_send()

    down, up = Gather(wd, ags, agr), Gather(wu, aus, aur)

    def merge_copy(i):
        ref, device = (
            lambda: (wm.at[d], right),
            lambda: (wm.at[d], left),
            lambda: (wm.at[d], other),
            lambda: (wm.at[d], mate),
            lambda: (wm.at[at(xl, c)], mate),
            lambda: (wm.at[at(xr, c)], mate),
            lambda: (wm.at[at(xo, c)], mate),
        )[i]()
        return rcopy(ref, ref, wms.at[i], wmr.at[i], device)

    def merge_arrival(i):
        ref = (
            lambda: wm.at[at(xl, c)],
            lambda: wm.at[at(xr, c)],
            lambda: wm.at[at(xo, c)],
            lambda: wm.at[at(x, 1 - c)],
            lambda: wm.at[at(xl, 1 - c)],
            lambda: wm.at[at(xr, 1 - c)],
            lambda: wm.at[at(xo, 1 - c)],
        )[i]()
        return rcopy(ref, ref, wms.at[i], wmr.at[i], mate)

    small[0]().wait()
    down.go(0, 1, 4)
    small[1]().wait()
    small[2]().wait()

    ss[...] = jnp.zeros_like(ss)

    def squares(q, carry):
        for copy in big(q):
            copy.wait()
        v = X[q].astype(F32)
        ss[...] += jnp.sum(v * v, -1, keepdims=True)
        return carry

    lax.fori_loop(0, nq, squares, 0)
    sc[...] = lax.rsqrt(ss[...] * (1.0 / width) + EPS)

    def normalise(q, carry):
        N[q] = (X[q].astype(F32) * sc[...] * gain_ref[q]).astype(BF)
        return carry

    lax.fori_loop(0, nq, normalise, 0)

    down.wait(0)
    down.go(2, 5)
    down.wait(1)
    down.go(3, 6)
    up.go(0, 1, 4)
    for i in range(4):
        merge_copy(i).start()

    small[3]().wait()
    small[4]().wait()
    query = jnp.concatenate([q_ref[...].astype(F32), jnp.zeros((TOK - q_ref.shape[0], q_ref.shape[1]), F32)], 0)
    query = query.astype(BF)
    for h in range(heads):
        lanes = slice(h * HEAD_DIM, (h + 1) * HEAD_DIM)
        scr[h * TOK:(h + 1) * TOK] = mm_nt(query[:, lanes], ek[:, lanes]) * HEAD_DIM ** (-0.5)
    scores = scr[...]
    weights = jnp.exp(scores - jnp.max(scores, -1, keepdims=True))
    scr[...] = weights / jnp.sum(weights, -1, keepdims=True)
    for h in range(heads):
        lanes = slice(h * HEAD_DIM, (h + 1) * HEAD_DIM)
        att[:, lanes] = mm(scr[h * TOK:(h + 1) * TOK].astype(BF), ev[:, lanes])

    down.wait(2, 3)
    down.go(7)
    down.wait(4, 5, 6, 7)

    inner[...] = jnp.zeros_like(inner)

    def add_inner(q, carry):
        inner[...] += mm(N[q], wd[q])
        return carry

    lax.fori_loop(0, nq, add_inner, 0)
    sig[...] = jax.nn.sigmoid(inner[...])
    hidden = inner[...] * sig[...]
    hid[...] = hidden.astype(BF)
    hidt[...] = hidden.T.astype(BF)

    bh[...] = jnp.zeros_like(bh)

    def fwd_send(q):
        return rcopy(O0.at[q], xin.at[q], zfs.at[q], zfr.at[q], (p + 1, d))

    def bwd_send(q):
        return rcopy(B0.at[q], G.at[q, pl.ds(0, s)], zbs.at[q], zbr.at[q], (p - 1, d))

    def fwd_block(j):
        return at((x + pick(j // 2, FWD)) % RING, jnp.where(j % 2 == 0, c, 1 - c))

    def bwd_block(j):
        return at((x + pick(j // 2, BWD)) % RING, jnp.where(j % 2 == 0, 1 - c, c))

    def first_forward(j, carry):
        q = fwd_block(j)

        @pl.when(j == 1)
        def _():
            up.wait(4)

        @pl.when(j == 2)
        def _():
            up.wait(0)
            up.go(2, 5)
            up.wait(1)
            up.go(3, 6)

        @pl.when(j == 3)
        def _():
            up.wait(5)

        @pl.when(j == 5)
        def _():
            up.wait(6)

        @pl.when(j == 6)
        def _():
            up.wait(2, 3)
            up.go(7)

        @pl.when(j == 7)
        def _():
            up.wait(7)

        out = (X[q, :s].astype(F32) + mm(hid[:s], wu[q])).astype(BF)

        @pl.when(last)
        def _():
            G[q, :s] = out
            G[q, s:] = (X[q, s:].astype(F32) + mm(hid[s:], wu[q])).astype(BF)

        @pl.when(jnp.logical_not(last))
        def _():
            O0[q] = out
            fwd_send(q).start()

        bh[...] += mm_nt(G[q, s:], wu[q])
        return carry

    lax.fori_loop(0, nq, first_forward, 0)

    for i, k in ((0, 4), (1, 5), (2, 6)):
        merge_arrival(i).wait_recv()
        merge_copy(k).start()

    def factor(rows):
        sg, inn = sig[rows], inner[rows]
        value = (bh[...] * sg * (1.0 + inn * (1.0 - sg))).astype(BF)
        wide = value.astype(F32)
        return value, wide, jnp.sum(wide * inn, -1, keepdims=True) * (1.0 / width)

    hi_rows, lo_rows = slice(s, 2 * s), slice(0, s)

    bu_b, wide_b, mean_b = factor(hi_rows)
    bu[...] = bu_b
    scale_b = sc[hi_rows]
    coef_b = scale_b * mean_b

    def first_backward(j, carry):
        q = bwd_block(j)
        back = mm_nt(bu[...], wd[q]) * gain_ref[q]
        value = G[q, s:].astype(F32) + scale_b * (back - X[q, s:].astype(F32) * coef_b)

        @pl.when(p > 0)
        def _():
            B0[q] = value.astype(BF)
            bwd_send(q).start()

        return carry

    lax.fori_loop(0, nq, first_backward, 0)

    for i in range(3, 7):
        merge_arrival(i).wait_recv()
    rows = att[...].astype(BF).astype(F32)
    scale_m = lax.rsqrt(jnp.mean(rows * rows, -1, keepdims=True) + EPS)
    rows = (rows * scale_m * mg_ref[...]).astype(BF)
    tokens = jax.nn.gelu(mm_nt(rows, wm[...].reshape(nq * wm.shape[1], wm.shape[2])))
    tk[p, :TOK] = tokens.astype(BF)
    slot = lax.broadcasted_iota(jnp.int32, (TOK, s), 0)
    place = lax.broadcasted_iota(jnp.int32, (TOK, s), 1)
    live = (slot < cnt_ref[0, 0]) & (place == off_ref[0, 0] + slot)
    tk[p, TOK:] = jnp.where(live, 1.0, 0.0).astype(BF)

    def tok_z(i, slot_z):
        ref = tk.at[y * Z + slot_z]
        return rcopy(ref, ref, tzs.at[i], tzr.at[i], (y * Z + (z + i) % Z, d))

    def tok_y(i, slot_y):
        ref = tk.at[pl.ds(slot_y * Z, Z)]
        return rcopy(ref, ref, tys.at[i], tyr.at[i], (((y + i) % n_y) * Z + z, d))

    for i in range(1, Z):
        tok_z(i, z).start()

    but_b = wide_b.T.astype(BF)
    bu[...] = but_b

    def down_mate(k):
        return rcopy(dps.at[k], dpr.at[k], dps_s.at[k], dps_r.at[k], mate)

    def down_x(k):
        device = (p, at((x + pick(k, BWD)) % RING, c))
        return rcopy(dxs.at[k], dxr.at[k], dxs_s.at[k], dxs_r.at[k], device)

    def up_mate(k):
        return rcopy(ups.at[k], upr.at[k], ups_s.at[k], ups_r.at[k], mate)

    def up_x(k):
        device = (p, at((x + pick(k, BWD)) % RING, c))
        return rcopy(uxs.at[k], uxr.at[k], uxs_s.at[k], uxs_r.at[k], device)

    def down_first(k, carry):
        dps[k] = mm(bu[...], N[bwd_block(2 * k), s:]).astype(BF)
        down_mate(k).start()
        return carry

    lax.fori_loop(0, RING, down_first, 0)

    def down_second(k, carry):
        value = mm(bu[...], N[bwd_block(2 * k + 1), s:])
        down_mate(k).wait_recv()
        value = value + dpr[k].astype(F32)

        @pl.when(k < RING - 1)
        def _():
            dxs[k] = value.astype(BF)
            down_x(k).start()

        @pl.when(k == RING - 1)
        def _():
            accd[...] = value

        return carry

    lax.fori_loop(0, RING, down_second, 0)

    def norm_copy(i):
        target = (d + i) % nq
        return rcopy(N.at[target, pl.ds(0, s)], nall.at[d], nas.at[i], nar.at[i], (p, target))

    def norm_arrival(i):
        ref = nall.at[(d + nq - i) % nq]
        return rcopy(ref, ref, nas.at[i], nar.at[i], mate)

    for i in range(1, nq):
        norm_copy(i).start()
    nall[d] = N[d, :s]

    for i in range(1, Z):
        tok_z(i, (z + Z - i) % Z).wait_recv()
    for i in range(1, n_y):
        tok_y(i, y).start()
    for i in range(1, n_y):
        tok_y(i, (y + n_y - i) % n_y).wait_recv()
    small[5]().wait()
    small[6]().wait()
    held = tk[:, :TOK].reshape(n_pipe * TOK, r)
    spots = tk[:, TOK:].reshape(n_pipe * TOK, s)
    vision = mm_tn(spots, held).astype(BF)
    marked = mm_tn(spots, jnp.ones_like(held))[:, :1] > 0.5
    fresh = jnp.where(marked, mm(vision, wv[...]), text[...].astype(F32)).astype(BF)

    def fresh_z(slot):
        return rcopy(fb, fra.at[y, slot], fzs.at[0], fzr.at[slot], (y * Z, d))

    def fresh_y(slot):
        return rcopy(fra.at[y], fra.at[slot], fys.at[0], fyr.at[slot], (0, d))

    @pl.when(z == 0)
    def _():
        fra[y, 0] = fresh

    @pl.when(z > 0)
    def _():
        fb[...] = fresh
        fresh_z(z).start()

    ss[...] = jnp.zeros_like(ss)
    ic[...] = jnp.zeros_like(ic)
    bh[...] = jnp.zeros_like(bh)

    def take_forward(q):
        v = xin[q].astype(F32)
        ss[:s] += jnp.sum(v * v, -1, keepdims=True)
        ic[...] += mm((v * gain_ref[q]).astype(BF), wd[q])

    def fwd_out(q):
        return pltpu.make_async_copy(xin.at[q], cols(fwd_h, q), outs.at[q])

    def bwd_out(q):
        return pltpu.make_async_copy(G.at[q, pl.ds(0, s)], cols(bwd_h, q), outs.at[nq + q])

    def but_copy(i):
        return rcopy(but.at[d], but.at[d], bus.at[i], bur.at[i], (p, (d + i) % nq))

    def but_arrival(i):
        ref = but.at[(d + nq - i) % nq]
        return rcopy(ref, ref, bus.at[i], bur.at[i], mate)

    def second(j, carry):
        qf, qb = fwd_block(j), bwd_block(j)

        @pl.when(p > 0)
        def _():
            fwd_send(qf).wait_recv()
            take_forward(qf)

        @pl.when((j == 1) & (z == 0))
        def _():
            for i in range(1, Z):
                fresh_z(i).wait_recv()

            @pl.when(y > 0)
            def _():
                fresh_y(y).start()

        @pl.when((j == nq - 1) & (p == 0))
        def _():
            for i in range(1, n_y):
                fresh_y(i).wait_recv()

            def assemble(q, carry):
                for i in range(per):
                    sec = q * per + i
                    xin[q, :, i * dp_cols:(i + 1) * dp_cols] = fra[sec // Z, sec % Z]
                take_forward(q)
                return carry

            lax.fori_loop(0, nq, assemble, 0)

        @pl.when(j == nq - 1)
        def _():
            scale = lax.rsqrt(ss[:s] * (1.0 / width) + EPS)
            hid2[...] = swish(ic[...] * scale).astype(BF)

            def finish(q, carry):
                xin[q] = (xin[q].astype(F32) + mm(hid2[...], wu[q])).astype(BF)
                fwd_out(q).start()
                return carry

            lax.fori_loop(0, nq, finish, 0)

        @pl.when(jnp.logical_not(last))
        def _():
            bwd_send(qb).wait_recv()

        bh[...] += mm_nt(G[qb, :s], wu[qb])

        @pl.when(j == nq - 1)
        def _():
            bu_a, wide_a, mean_a = factor(lo_rows)
            but[d] = wide_a.T.astype(BF)
            for i in range(1, nq):
                but_copy(i).start()
            bu[...] = bu_a
            ss[:s] = mean_a

        k = j // 2
        term = mm(hidt[...], G[qb])

        @pl.when(j % 2 == 0)
        def _():
            ups[k] = term.astype(BF)
            up_mate(k).start()

        @pl.when(j % 2 == 1)
        def _():
            upf[...] = term
            up_mate(k).wait_recv()
            total = upf[...] + upr[k].astype(F32)

            @pl.when(k < RING - 1)
            def _():
                uxs[k] = total.astype(BF)
                up_x(k).start()

            @pl.when(k == RING - 1)
            def _():
                accu[...] = total

        return carry

    lax.fori_loop(0, nq, second, 0)

    scale_a = sc[lo_rows]
    coef_a = scale_a * ss[:s]

    def second_backward(q, carry):
        back = mm_nt(bu[...], wd[q]) * gain_ref[q]
        value = G[q, :s].astype(F32) + scale_a * (back - X[q, :s].astype(F32) * coef_a)
        G[q, :s] = value.astype(BF)
        bwd_out(q).start()
        return carry

    lax.fori_loop(0, nq, second_backward, 0)

    for k in range(RING - 1):
        up_x(k).wait_recv()
        accu[...] += uxr[k].astype(F32)
    up_out = pltpu.make_async_copy(accu, gu_h, outs.at[2 * nq])
    up_out.start()
    for k in range(RING - 1):
        down_x(k).wait_recv()
        accd[...] += dxr[k].astype(F32)
    for i in range(1, nq):
        norm_arrival(i).wait_recv()
        but_arrival(i).wait_recv()

    def add_down(q, carry):
        accd[...] += mm(but[q], nall[q])
        return carry

    lax.fori_loop(0, nq, add_down, 0)
    gdo[...] = accd[...].T
    down_out = pltpu.make_async_copy(gdo, gd_h, outs.at[2 * nq + 1])
    down_out.start()

    down.drain()
    up.drain()
    for i in range(7):
        merge_copy(i).wait_send()
    for i in range(1, Z):
        tok_z(i, z).wait_send()
    for i in range(1, n_y):
        tok_y(i, y).wait_send()

    @pl.when(z > 0)
    def _():
        fresh_z(z).wait_send()

    @pl.when((z == 0) & (y > 0))
    def _():
        fresh_y(y).wait_send()

    for i in range(1, nq):
        norm_copy(i).wait_send()
        but_copy(i).wait_send()
    for k in range(RING):
        up_mate(k).wait_send()
        down_mate(k).wait_send()
    for k in range(RING - 1):
        up_x(k).wait_send()
        down_x(k).wait_send()

    def drain(q, carry):
        @pl.when(jnp.logical_not(last))
        def _():
            fwd_send(q).wait_send()

        @pl.when(p > 0)
        def _():
            bwd_send(q).wait_send()

        fwd_out(q).wait()
        bwd_out(q).wait()
        return carry

    lax.fori_loop(0, nq, drain, 0)
    up_out.wait()
    down_out.wait()


def body(
    n_pipe, nq,
    act_in, stash_a, grad_in, text_emb, enc_query, enc_key, enc_value, tok_count, tok_offset,
    merge_gain, w_merge, w_vision, norm_gain, w_down, w_up,
):
    s, width = act_in.shape[2:]
    db, r = w_down.shape[1:]
    enc = enc_query.shape[2]
    heads = enc // HEAD_DIM
    cols = w_vision.shape[1]
    img = enc_key.shape[1]
    n_y = n_pipe // Z
    vm = pltpu.VMEM
    dma = lambda n: pltpu.SemaphoreType.DMA((n,))
    any_spec = pl.BlockSpec(memory_space=pl.ANY)
    vmem_spec = pl.BlockSpec(memory_space=pltpu.VMEM)
    smem_spec = pl.BlockSpec(memory_space=pltpu.SMEM)
    scratch = [
        vm((nq, 2 * s, db), BF),
        vm((nq, 2 * s, db), BF),
        vm((nq, 2 * s, db), BF),
        vm((nq, db, r), BF),
        vm((nq, r, db), BF),
        vm((nq, s, db), BF),
        vm((nq, s, db), BF),
        vm((nq, s, db), BF),
        vm((nq, s, db), BF),
        vm((nq, r, s), BF),
        vm((r, db), F32),
        vm((RING, r, db), BF), vm((RING, r, db), BF), vm((RING, r, db), BF), vm((RING, r, db), BF),
        vm((RING, r, db), BF), vm((RING, r, db), BF), vm((RING, r, db), BF), vm((RING, r, db), BF),
        vm((r, db), F32), vm((r, db), F32),
        vm((nq, r // nq, enc), BF),
        vm((img, enc), BF), vm((img, enc), BF),
        vm((s, cols), BF), vm((r, cols), BF),
        vm((heads * TOK, img), F32),
        vm((TOK, enc), F32),
        vm((n_pipe, 2 * TOK, r), BF),
        vm((s, cols), BF),
        vm((n_y, Z, s, cols), BF),
        vm((2 * s, 1), F32),
        vm((2 * s, r), F32), vm((2 * s, r), F32),
        vm((2 * s, r), BF), vm((r, 2 * s), BF),
        vm((s, r), F32), vm((s, r), BF),
        vm((s, r), F32),
        vm((2 * s, 1), F32),
        vm((s, r), BF),
        vm((db, r), F32),
        dma(8 + 3 * nq),
        dma(8), dma(8), dma(8), dma(8), dma(7), dma(7),
        dma(nq), dma(nq), dma(nq), dma(nq),
        dma(nq), dma(nq), dma(nq), dma(nq),
        dma(RING), dma(RING), dma(RING), dma(RING),
        dma(RING), dma(RING), dma(RING), dma(RING),
        dma(Z), dma(Z), dma(n_y), dma(n_y),
        dma(1), dma(Z), dma(1), dma(n_y),
        dma(2 * nq + 2),
    ]
    fwd, bwd, grad_down, grad_up = pl.pallas_call(
        functools.partial(kernel, n_pipe),
        out_shape=(
            jax.ShapeDtypeStruct((s, width), BF),
            jax.ShapeDtypeStruct((s, width), BF),
            jax.ShapeDtypeStruct((db, r), F32),
            jax.ShapeDtypeStruct((r, db), F32),
        ),
        in_specs=[
            any_spec, any_spec, any_spec, any_spec, any_spec, vmem_spec, any_spec, any_spec,
            smem_spec, smem_spec, vmem_spec, any_spec, vmem_spec, any_spec, any_spec,
        ],
        out_specs=(any_spec,) * 4,
        scratch_shapes=scratch,
        compiler_params=pltpu.CompilerParams(
            collective_id=0, has_side_effects=True, vmem_limit_bytes=56 * 2**20
        ),
        name="relay",
    )(
        act_in[0, 0], stash_a[0, 0], grad_in[0, 0], text_emb[0], w_vision,
        enc_query[0], enc_key[0], enc_value[0], tok_count, tok_offset,
        merge_gain[None], w_merge.T, norm_gain.reshape(nq, 1, db), w_down[0], w_up[0],
    )
    return fwd[None, None], bwd[None, None], grad_down[None], grad_up[None]


def solution(mesh):
    in_specs = (
        P("dp", "pipe", None, None),
        P("dp", "pipe", None, None),
        P("dp", "pipe", None, None),
        P("dp", None, "pipe"),
        P("dp", "pipe", None),
        P("dp", "pipe", None),
        P("dp", "pipe", None),
        P("dp", "pipe"),
        P("dp", "pipe"),
        P(),
        P(None, "dp"),
        P(None, "pipe"),
        P("pipe", None),
        P("pipe", "dp", None),
        P("pipe", None, "dp"),
    )
    out_specs = (
        P("dp", "pipe", None, None),
        P("dp", "pipe", None, None),
        P("pipe", "dp", None),
        P("pipe", None, "dp"),
    )
    step = functools.partial(body, mesh.shape["pipe"], mesh.shape["dp"])
    return jax.shard_map(step, mesh=mesh, in_specs=in_specs, out_specs=out_specs, check_vma=False)
```

```python
import functools

import jax
import jax.numpy as jnp
from jax import lax
from jax.experimental import pallas as pl
from jax.experimental.pallas import tpu as pltpu
from jax.sharding import PartitionSpec as P

HEAD_DIM = 128
EPS = 1e-06
RING = 4
Z = 8
VM = 56
TOK = 16
MESH = pl.DeviceIdType.MESH
BF, F32 = jnp.bfloat16, jnp.float32


def mm(a, b):
    return jnp.dot(a, b, preferred_element_type=F32)


def mm_nt(a, b):
    return lax.dot_general(a, b, (((1,), (1,)), ((), ())), preferred_element_type=F32)


def mm_tn(a, b):
    return lax.dot_general(a, b, (((0,), (0,)), ((), ())), preferred_element_type=F32)


def swish(inner):
    return inner * jax.nn.sigmoid(inner)


def pick(k, values):
    out = jnp.int32(values[-1])
    for i in range(len(values) - 2, -1, -1):
        out = jnp.where(k == i, jnp.int32(values[i]), out)
    return out


def rcopy(src, dst, send_sem, recv_sem, device):
    return pltpu.make_async_remote_copy(
        src_ref=src,
        dst_ref=dst,
        send_sem=send_sem,
        recv_sem=recv_sem,
        device_id=device,
        device_id_type=MESH,
    )


FWD = (0, 3, 1, 2)
BWD = (2, 1, 3, 0)


def kernel(
    n_pipe,
    act_h, st_h, gin_h, text_h, wv_h, q_ref, ek_h, ev_h, cnt_ref, off_ref, mg_ref, wm_h, gain_ref, wd_h, wu_h,
    fwd_h, bwd_h, gd_h, gu_h,
    X, G, N, wd, wu, xin, O0, B0, nall, but, ups, upr, uxs, uxr, dps, dpr, dxs, dxr, accu, accd,
    wm, ek, ev, text, wv, scr, att, tk, fb, fra, rx, ru, rh, rg, rst, rwd, rgn, rb, rp, pk, sc, inner, sig, hid, hidt, bh, bu, bu2, ic, ss, hid2, gdo,
    ld, ags, agr, aus, aur, wms, wmr, zfs, zfr, zbs, zbr, nas, nar, bus, bur,
    ups_s, ups_r, uxs_s, uxs_r, dps_s, dps_r, dxs_s, dxs_r, tzs, tzr, tys, tyr, fzs, fzr, fys, fyr, rfs, rfr, rbs, rbr, outs,
):
    nq, s2, db = X.shape
    s = s2 // 2
    r = wu.shape[1]
    dp_cols = fb.shape[1]
    per = db // dp_cols
    n_y = n_pipe // Z
    width = nq * db
    heads = att.shape[1] // HEAD_DIM

    p, d = lax.axis_index("pipe"), lax.axis_index("dp")
    y, z = p // Z, p % Z
    x, c = d // 2, d % 2
    last = p == n_pipe - 1
    xr, xl, xo = (x + 1) % RING, (x + 3) % RING, (x + 2) % RING

    def at(chip, core):
        return chip * 2 + core

    right, left, other, mate = (p, at(xr, c)), (p, at(xl, c)), (p, at(xo, c)), (p, at(x, 1 - c))

    def cols(ref, q):
        return ref.at[:, pl.ds(pl.multiple_of(q * db, 128), db)]

    def load(i, src, dst):
        return pltpu.make_async_copy(src, dst, ld.at[i])

    small = [
        lambda: load(0, wd_h, wd.at[d]),
        lambda: load(1, wu_h, wu.at[d]),
        lambda: load(2, wm_h, wm.at[d]),
        lambda: load(3, ek_h, ek),
        lambda: load(4, ev_h, ev),
        lambda: load(5, text_h, text),
        lambda: load(6, wv_h, wv),
    ]

    def big(q):
        return (
            load(8 + q, cols(act_h, q), X.at[q, pl.ds(0, s)]),
            load(8 + nq + q, cols(st_h, q), X.at[q, pl.ds(s, s)]),
            load(8 + 2 * nq + q, cols(gin_h, q), G.at[q, pl.ds(s, s)]),
        )

    for copy in small:
        copy().start()

    def start_big(q, carry):
        for copy in big(q):
            copy.start()
        return carry

    lax.fori_loop(0, nq, start_big, 0)

    barrier = pltpu.get_barrier_semaphore()

    def greet(device):
        pl.semaphore_signal(barrier, inc=1, device_id=device, device_id_type=MESH)

    for i in range(1, nq):
        greet((p, (d + i) % nq))
    for i in range(1, Z):
        greet((y * Z + (z + i) % Z, d))
    for i in range(1, n_y):
        greet((((y + i) % n_y) * Z + z, d))
    up_wrap = (z == Z - 1) & (y < n_y - 1)
    down_wrap = (z == 0) & (y > 0)

    @pl.when(up_wrap)
    def _():
        greet((p + 1, d))

    @pl.when(down_wrap)
    def _():
        greet((p - 1, d))

    extra = jnp.where(up_wrap | down_wrap, 1, 0)
    pl.semaphore_wait(barrier, nq - 1 + Z - 1 + n_y - 1 + extra)

    class Gather:
        def __init__(self, buf, send, recv):
            self.buf, self.send, self.recv = buf, send, recv
            self.half = buf.shape[1] // 2

        def copy(self, i):
            lo, hi = pl.ds(0, self.half), pl.ds(self.half, self.half)
            ref, device = (
                lambda: (self.buf.at[d], right),
                lambda: (self.buf.at[d], left),
                lambda: (self.buf.at[at(xl, c), lo], right),
                lambda: (self.buf.at[at(xr, c), hi], left),
                lambda: (self.buf.at[d], mate),
                lambda: (self.buf.at[at(xl, c)], mate),
                lambda: (self.buf.at[at(xr, c)], mate),
                lambda: (self.buf.at[at(xo, c)], mate),
            )[i]()
            return rcopy(ref, ref, self.send.at[i], self.recv.at[i], device)

        def arrival(self, i):
            lo, hi = pl.ds(0, self.half), pl.ds(self.half, self.half)
            ref = (
                lambda: self.buf.at[at(xl, c)],
                lambda: self.buf.at[at(xr, c)],
                lambda: self.buf.at[at(xo, c), lo],
                lambda: self.buf.at[at(xo, c), hi],
                lambda: self.buf.at[at(x, 1 - c)],
                lambda: self.buf.at[at(xl, 1 - c)],
                lambda: self.buf.at[at(xr, 1 - c)],
                lambda: self.buf.at[at(xo, 1 - c)],
            )[i]()
            return rcopy(ref, ref, self.send.at[i], self.recv.at[i], mate)

        def go(self, *which):
            for i in which:
                self.copy(i).start()

        def wait(self, *which):
            for i in which:
                self.arrival(i).wait_recv()

        def drain(self):
            for i in range(8):
                self.copy(i).wait_send()

    down, up = Gather(wd, ags, agr), Gather(wu, aus, aur)

    def merge_copy(i):
        ref, device = (
            lambda: (wm.at[d], right),
            lambda: (wm.at[d], left),
            lambda: (wm.at[d], other),
            lambda: (wm.at[d], mate),
            lambda: (wm.at[at(xl, c)], mate),
            lambda: (wm.at[at(xr, c)], mate),
            lambda: (wm.at[at(xo, c)], mate),
        )[i]()
        return rcopy(ref, ref, wms.at[i], wmr.at[i], device)

    def merge_arrival(i):
        ref = (
            lambda: wm.at[at(xl, c)],
            lambda: wm.at[at(xr, c)],
            lambda: wm.at[at(xo, c)],
            lambda: wm.at[at(x, 1 - c)],
            lambda: wm.at[at(xl, 1 - c)],
            lambda: wm.at[at(xr, 1 - c)],
            lambda: wm.at[at(xo, 1 - c)],
        )[i]()
        return rcopy(ref, ref, wms.at[i], wmr.at[i], mate)

    def tok_z(i, slot_z):
        ref = tk.at[y * Z + slot_z]
        return rcopy(ref, ref, tzs.at[i], tzr.at[i], (y * Z + (z + i) % Z, d))

    def tok_y(i, slot_y):
        ref = tk.at[pl.ds(slot_y * Z, Z)]
        return rcopy(ref, ref, tys.at[i], tyr.at[i], (((y + i) % n_y) * Z + z, d))

    def fresh_z(slot):
        return rcopy(fb, fra.at[y, slot], fzs.at[0], fzr.at[slot], (y * Z, d))

    def fresh_y(slot):
        target = jnp.where(y == n_y - 1, 0, y - 1) * Z
        return rcopy(fra.at[slot], fra.at[slot], fys.at[slot], fyr.at[slot], (target, d))

    def fwd_send(q):
        return rcopy(O0.at[q], xin.at[q], zfs.at[q], zfr.at[q], (p + 1, d))

    def bwd_send(q):
        return rcopy(B0.at[q], G.at[q, pl.ds(0, s)], zbs.at[q], zbr.at[q], (p - 1, d))

    def raw_f(i):
        src, dst = (
            lambda: (X.at[d, pl.ds(0, s)], rx),
            lambda: (wu.at[d], ru),
            lambda: (hid.at[pl.ds(0, s)], rh),
        )[i]()
        return rcopy(src, dst, rfs.at[i], rfr.at[i], (p + 1, d))

    def raw_b(i):
        src, dst = (
            lambda: (X.at[d, pl.ds(s, s)], rst),
            lambda: (G.at[d, pl.ds(s, s)], rg),
            lambda: (wd.at[d], rwd),
            lambda: (gain_ref.at[d], rgn),
            lambda: (bu, rb.at[pl.ds(0, s)]),
            lambda: (pk, rp),
            lambda: (hid.at[pl.ds(s, s)], rb.at[pl.ds(s, s)]),
        )[i]()
        return rcopy(src, dst, rbs.at[i], rbr.at[i], (p - 1, d))

    def raw_u():
        return rcopy(wu.at[d], rg, rbs.at[1], rbr.at[1], (p - 1, d))

    inside = jnp.logical_not(last)

    def fwd_block(j):
        return at((x + pick(j // 2, FWD)) % RING, jnp.where(j % 2 == 0, c, 1 - c))

    def bwd_block(j):
        return at((x + pick(j // 2, BWD)) % RING, jnp.where(j % 2 == 0, 1 - c, c))

    def down_mate(k):
        return rcopy(dps.at[k], dpr.at[k], dps_s.at[k], dps_r.at[k], mate)

    def down_x(k):
        device = (p, at((x + pick(k, BWD)) % RING, c))
        return rcopy(dxs.at[k], dxr.at[k], dxs_s.at[k], dxs_r.at[k], device)

    def up_mate(k):
        return rcopy(ups.at[k], upr.at[k], ups_s.at[k], ups_r.at[k], mate)

    def up_x(k):
        device = (p, at((x + pick(k, BWD)) % RING, c))
        return rcopy(uxs.at[k], uxr.at[k], uxs_s.at[k], uxs_r.at[k], device)

    def norm_copy(i):
        target = (d + i) % nq
        return rcopy(N.at[target, pl.ds(0, s)], nall.at[d], nas.at[i], nar.at[i], (p, target))

    def norm_arrival(i):
        ref = nall.at[(d + nq - i) % nq]
        return rcopy(ref, ref, nas.at[i], nar.at[i], mate)

    def but_copy(i):
        return rcopy(but.at[d], but.at[d], bus.at[i], bur.at[i], (p, (d + i) % nq))

    def but_arrival(i):
        ref = but.at[(d + nq - i) % nq]
        return rcopy(ref, ref, bus.at[i], bur.at[i], mate)

    def fwd_out(q):
        return pltpu.make_async_copy(xin.at[q], cols(fwd_h, q), outs.at[q])

    def bwd_out(q):
        return pltpu.make_async_copy(G.at[q, pl.ds(0, s)], cols(bwd_h, q), outs.at[nq + q])

    def each(n, step):
        def run(i, carry):
            step(i)
            return carry

        lax.fori_loop(0, n, run, 0, unroll=True)

    small[2]().wait()
    for i in range(4):
        merge_copy(i).start()
    small[0]().wait()
    small[1]().wait()
    down.go(0, 1, 4)
    up.go(0, 1, 4)

    for copy in big(d):
        copy.wait()

    @pl.when(inside)
    def _():
        raw_f(0).start()
        raw_f(1).start()

    @pl.when(p > 0)
    def _():
        raw_b(0).start()

    @pl.when((p > 0) & inside)
    def _():
        raw_b(1).start()

    @pl.when(last)
    def _():
        raw_u().start()

    small[3]().wait()
    small[4]().wait()
    query = jnp.concatenate([q_ref[...].astype(F32), jnp.zeros((TOK - q_ref.shape[0], q_ref.shape[1]), F32)], 0)
    query = query.astype(BF)
    for h in range(heads):
        lanes = slice(h * HEAD_DIM, (h + 1) * HEAD_DIM)
        scr[h * TOK:(h + 1) * TOK] = mm_nt(query[:, lanes], ek[:, lanes]) * HEAD_DIM ** (-0.5)
    scores = scr[...]
    weights = jnp.exp(scores - jnp.max(scores, -1, keepdims=True))
    scr[...] = weights / jnp.sum(weights, -1, keepdims=True)
    for h in range(heads):
        lanes = slice(h * HEAD_DIM, (h + 1) * HEAD_DIM)
        att[:, lanes] = mm(scr[h * TOK:(h + 1) * TOK].astype(BF), ev[:, lanes])

    def wait_big(i, carry):
        for copy in big((d + i) % nq):
            copy.wait()
        return carry

    lax.fori_loop(1, nq, wait_big, 0)
    ss[...] = jnp.zeros_like(ss)

    def squares(q):
        v = X[q].astype(F32)
        ss[...] += jnp.sum(v * v, -1, keepdims=True)

    each(nq, squares)
    sc[...] = lax.rsqrt(ss[...] * (1.0 / width) + EPS)

    def normalise(q):
        N[q] = (X[q].astype(F32) * sc[...] * gain_ref[q]).astype(BF)

    each(nq, normalise)

    for i, k in ((0, 4), (1, 5), (2, 6)):
        merge_arrival(i).wait_recv()
        merge_copy(k).start()
    for i in range(3, 7):
        merge_arrival(i).wait_recv()
    rows = att[...].astype(BF).astype(F32)
    scale_m = lax.rsqrt(jnp.mean(rows * rows, -1, keepdims=True) + EPS)
    rows = (rows * scale_m * mg_ref[...][None, :]).astype(BF)
    tokens = jax.nn.gelu(mm_nt(rows, wm[...].reshape(nq * wm.shape[1], wm.shape[2])))
    tk[p, :TOK] = tokens.astype(BF)
    slot = lax.broadcasted_iota(jnp.int32, (TOK, s), 0)
    place = lax.broadcasted_iota(jnp.int32, (TOK, s), 1)
    live = (slot < cnt_ref[0, 0]) & (place == off_ref[0, 0] + slot)
    tk[p, TOK:] = jnp.where(live, 1.0, 0.0).astype(BF)
    for i in range(1, Z):
        tok_z(i, z).start()

    @pl.when(p > 0)
    def _():
        raw_b(2).start()
        raw_b(3).start()

    down.wait(0)
    down.go(2, 5)
    down.wait(1)
    down.go(3, 6)
    up.wait(0)
    up.go(2, 5)
    up.wait(1)
    up.go(3, 6)

    for i in range(1, Z):
        tok_z(i, (z + Z - i) % Z).wait_recv()
    for i in range(1, n_y):
        tok_y(i, y).start()
    down.wait(2, 3)
    down.go(7)
    down.wait(4, 5, 6, 7)

    total = mm(N[0], wd[0])
    for q in range(1, nq):
        total += mm(N[q], wd[q])
    inner[...] = total
    sig[...] = jax.nn.sigmoid(total)
    hidden = total * sig[...]
    hid[...] = hidden.astype(BF)
    hidt[...] = hidden.T.astype(BF)

    @pl.when(inside)
    def _():
        raw_f(2).start()

    @pl.when(last)
    def _():
        raw_b(6).start()


    for i in range(1, n_y):
        tok_y(i, (y + n_y - i) % n_y).wait_recv()

    small[5]().wait()
    small[6]().wait()
    held = tk[:, :TOK].reshape(n_pipe * TOK, r)
    spots = tk[:, TOK:].reshape(n_pipe * TOK, s)
    vision = mm_tn(spots, held).astype(BF)
    marked = mm_tn(spots, jnp.ones_like(held))[:, :1] > 0.5
    fresh = jnp.where(marked, mm(vision, wv[...]), text[...].astype(F32)).astype(BF)

    @pl.when(z == 0)
    def _():
        fra[y, 0] = fresh

    @pl.when(z > 0)
    def _():
        fb[...] = fresh
        fresh_z(z).start()

    bh[...] = jnp.zeros_like(bh)
    for k in range(RING):
        if k == RING - 1:
            up.wait(2, 3)
            up.go(7)
            for i in range(1, nq):
                norm_copy(i).start()
            nall[d] = N[d, :s]

            @pl.when(z == 0)
            def _():
                for i in range(1, Z):
                    fresh_z(i).wait_recv()

                @pl.when(y > 0)
                def _():
                    fresh_y(y).start()

        up.wait(4 + k)
        pair = [fwd_block(2 * k), fwd_block(2 * k + 1)]
        sent = pair[1:] if k == 0 else pair
        for q in pair:
            O0[q] = (X[q, :s].astype(F32) + mm(hid[:s], wu[q])).astype(BF)

        @pl.when(last)
        def _():
            for q in pair:
                G[q, :s] = O0[q]
                G[q, s:] = (X[q, s:].astype(F32) + mm(hid[s:], wu[q])).astype(BF)

        @pl.when(inside)
        def _():
            for q in sent:
                fwd_send(q).start()

        bh[...] += mm_nt(G[pair[0], s:], wu[pair[0]]) + mm_nt(G[pair[1], s:], wu[pair[1]])

    def factor(rows):
        sg, inn = sig[rows], inner[rows]
        value = (bh[...] * sg * (1.0 + inn * (1.0 - sg))).astype(BF)
        wide = value.astype(F32)
        return value, wide, jnp.sum(wide * inn, -1, keepdims=True) * (1.0 / width)

    hi_rows, lo_rows = slice(s, 2 * s), slice(0, s)

    bu_b, wide_b, mean_b = factor(hi_rows)
    bu[...] = bu_b
    scale_b = sc[hi_rows]
    coef_b = scale_b * mean_b
    columns = jnp.concatenate([jnp.broadcast_to(scale_b, (s, 8)), jnp.broadcast_to(coef_b, (s, s - 8))], 1).T
    pk[...] = columns[4:12]

    @pl.when(p > 0)
    def _():
        raw_b(4).start()
        raw_b(5).start()

    for first in range(0, nq - 1, 4):
        group = [bwd_block(j) for j in range(first, min(first + 4, nq - 1))]
        for q in group:
            back = mm_nt(bu[...], wd[q]) * gain_ref[q]
            value = G[q, s:].astype(F32) + scale_b * (back - X[q, s:].astype(F32) * coef_b)
            B0[q] = value.astype(BF)

        @pl.when(p > 0)
        def _():
            for q in group:
                bwd_send(q).start()

    turned = wide_b.T.astype(BF)
    for k in range(RING):
        dps[k] = mm(turned, N[bwd_block(2 * k), s:]).astype(BF)
    for k in range(RING):
        down_mate(k).start()
    for k in range(RING):
        down_mate(k).wait_recv()
    for k in range(RING):
        value = mm(turned, N[bwd_block(2 * k + 1), s:]) + dpr[k].astype(F32)
        if k < RING - 1:
            dxs[k] = value.astype(BF)
        else:
            accd[...] = value
    for k in range(RING - 1):
        down_x(k).start()

    ss[...] = jnp.zeros_like(ss)
    ic[...] = jnp.zeros_like(ic)
    bh[...] = jnp.zeros_like(bh)

    def take_forward(q):
        v = xin[q].astype(F32)
        ss[:s] += jnp.sum(v * v, -1, keepdims=True)
        ic[...] += mm((v * gain_ref[q]).astype(BF), wd[q])

    def second(j, carry):
        qf, qb = fwd_block(j), jnp.where(j == 0, d, bwd_block(j - 1))

        for i in range(2, n_y - 1):

            @pl.when((z == 0) & (j == 2 * i - 3) & (y <= n_y - 1 - i) & (y > 0))
            def _():
                fresh_y(y + i - 1).wait_recv()
                fresh_y(y + i - 1).start()

        @pl.when((p > 0) & (j > 0))
        def _():
            fwd_send(qf).wait_recv()

        @pl.when((p > 0) & (j == 0))
        def _():
            for i in range(3):
                raw_f(i).wait_recv()
            xin[d] = (rx[...].astype(F32) + mm(rh[...], ru[...])).astype(BF)

        @pl.when(p > 0)
        def _():
            take_forward(qf)

        @pl.when((j == nq - 1) & (p == 0))
        def _():
            for i in range(1, n_y):
                fresh_y(i).wait_recv()

            def assemble(q):
                for i in range(per):
                    sec = q * per + i
                    xin[q, :, i * dp_cols:(i + 1) * dp_cols] = fra[sec // Z, sec % Z]
                take_forward(q)

            each(nq, assemble)

        @pl.when(j == nq - 1)
        def _():
            scale = lax.rsqrt(ss[:s] * (1.0 / width) + EPS)
            hid2[...] = swish(ic[...] * scale).astype(BF)

            def finish(q):
                xin[q] = (xin[q].astype(F32) + mm(hid2[...], wu[q])).astype(BF)

            each(nq, finish)
            for q in range(nq):
                fwd_out(q).start()

        @pl.when(inside & (j > 0))
        def _():
            bwd_send(qb).wait_recv()

        @pl.when(inside & (j == 0))
        def _():
            for i in range(6):
                raw_b(i).wait_recv()

        @pl.when((p == n_pipe - 2) & (j == 0))
        def _():
            raw_b(6).wait_recv()
            rg[...] = (rst[...].astype(F32) + mm(rb[s:], rg[...])).astype(BF)

        @pl.when(inside & (j == 0))
        def _():
            wide = jnp.concatenate([rp[...], jnp.zeros((s - 8, s), F32)], 0).T
            back = mm_nt(rb[:s], rwd[...]) * rgn[...]
            value = rg[...].astype(F32) + wide[:, 0:1] * (back - rst[...].astype(F32) * wide[:, 4:5])
            G[d, :s] = value.astype(BF)

        bh[...] += mm_nt(G[qb, :s], wu[qb])

        @pl.when(j == nq - 1)
        def _():
            bu_a, wide_a, mean_a = factor(lo_rows)
            but[d] = wide_a.T.astype(BF)
            for i in range(1, nq):
                but_copy(i).start()
            bu2[...] = bu_a
            ss[:s] = mean_a

        term = mm(hidt[...], G[qb])

        @pl.when(j == 0)
        def _():
            accu[...] = term

        @pl.when(j % 2 == 1)
        def _():
            ups[j // 2] = term.astype(BF)
            up_mate(j // 2).start()

        @pl.when((j % 2 == 0) & (j > 0))
        def _():
            k = j // 2 - 1
            up_mate(k).wait_recv()
            uxs[k] = (term + upr[k].astype(F32)).astype(BF)
            up_x(k).start()

        return carry

    lax.fori_loop(0, nq, second, 0)

    scale_a = sc[lo_rows]
    coef_a = scale_a * ss[:s]

    def second_backward(q):
        back = mm_nt(bu2[...], wd[q]) * gain_ref[q]
        value = G[q, :s].astype(F32) + scale_a * (back - X[q, :s].astype(F32) * coef_a)
        G[q, :s] = value.astype(BF)

    each(nq, second_backward)
    for q in range(nq):
        bwd_out(q).start()

    for k in range(RING - 1):
        up_x(k).wait_recv()
    up_mate(RING - 1).wait_recv()
    total = accu[...] + upr[RING - 1].astype(F32)
    for k in range(RING - 1):
        total += uxr[k].astype(F32)
    accu[...] = total
    up_out = pltpu.make_async_copy(accu, gu_h, outs.at[2 * nq])
    up_out.start()
    for k in range(RING - 1):
        down_x(k).wait_recv()
    for i in range(1, nq):
        norm_arrival(i).wait_recv()
        but_arrival(i).wait_recv()
    total = accd[...]
    for k in range(RING - 1):
        total += dxr[k].astype(F32)
    for q in range(nq):
        total += mm(but[q], nall[q])
    gdo[...] = total.T
    down_out = pltpu.make_async_copy(gdo, gd_h, outs.at[2 * nq + 1])
    down_out.start()

    down.drain()
    up.drain()
    for i in range(7):
        merge_copy(i).wait_send()
    for i in range(1, Z):
        tok_z(i, z).wait_send()
    for i in range(1, n_y):
        tok_y(i, y).wait_send()

    @pl.when(z > 0)
    def _():
        fresh_z(z).wait_send()

    @pl.when((z == 0) & (y > 0))
    def _():
        fresh_y(y).wait_send()
        for i in range(2, n_y - 1):

            @pl.when(y <= n_y - 1 - i)
            def _():
                fresh_y(y + i - 1).wait_send()

    for i in range(1, nq):
        norm_copy(i).wait_send()
        but_copy(i).wait_send()
    for k in range(RING):
        up_mate(k).wait_send()
        down_mate(k).wait_send()
    for k in range(RING - 1):
        up_x(k).wait_send()
        down_x(k).wait_send()

    def drain(q, carry):
        @pl.when(inside & (q != d))
        def _():
            fwd_send(q).wait_send()

        @pl.when((p > 0) & (q != d))
        def _():
            bwd_send(q).wait_send()

        fwd_out(q).wait()
        bwd_out(q).wait()
        return carry

    lax.fori_loop(0, nq, drain, 0)

    @pl.when(inside)
    def _():
        for i in range(3):
            raw_f(i).wait_send()

    @pl.when(p > 0)
    def _():
        for i in range(6):
            raw_b(i).wait_send()

    @pl.when(last)
    def _():
        raw_b(6).wait_send()

    up_out.wait()
    down_out.wait()


def body(
    n_pipe, nq,
    act_in, stash_a, grad_in, text_emb, enc_query, enc_key, enc_value, tok_count, tok_offset,
    merge_gain, w_merge, w_vision, norm_gain, w_down, w_up,
):
    s, width = act_in.shape[2:]
    db, r = w_down.shape[1:]
    enc = enc_query.shape[2]
    heads = enc // HEAD_DIM
    cols = w_vision.shape[1]
    img = enc_key.shape[1]
    n_y = n_pipe // Z
    vm = pltpu.VMEM
    dma = lambda n: pltpu.SemaphoreType.DMA((n,))
    any_spec = pl.BlockSpec(memory_space=pl.ANY)
    vmem_spec = pl.BlockSpec(memory_space=pltpu.VMEM)
    smem_spec = pl.BlockSpec(memory_space=pltpu.SMEM)
    scratch = [
        vm((nq, 2 * s, db), BF),
        vm((nq, 2 * s, db), BF),
        vm((nq, 2 * s, db), BF),
        vm((nq, db, r), BF),
        vm((nq, r, db), BF),
        vm((nq, s, db), BF),
        vm((nq, s, db), BF),
        vm((nq, s, db), BF),
        vm((nq, s, db), BF),
        vm((nq, r, s), BF),
        vm((RING, r, db), BF), vm((RING, r, db), BF), vm((RING, r, db), BF), vm((RING, r, db), BF),
        vm((RING, r, db), BF), vm((RING, r, db), BF), vm((RING, r, db), BF), vm((RING, r, db), BF),
        vm((r, db), F32), vm((r, db), F32),
        vm((nq, r // nq, enc), BF),
        vm((img, enc), BF), vm((img, enc), BF),
        vm((s, cols), BF), vm((r, cols), BF),
        vm((heads * TOK, img), F32),
        vm((TOK, enc), F32),
        vm((n_pipe, 2 * TOK, r), BF),
        vm((s, cols), BF),
        vm((n_y, Z, s, cols), BF),
        vm((s, db), BF), vm((r, db), BF), vm((s, r), BF),
        vm((s, db), BF), vm((s, db), BF), vm((db, r), BF), vm((1, db), F32),
        vm((2 * s, r), BF), vm((8, s), F32),
        vm((8, s), F32),
        vm((2 * s, 1), F32),
        vm((2 * s, r), F32), vm((2 * s, r), F32),
        vm((2 * s, r), BF), vm((r, 2 * s), BF),
        vm((s, r), F32), vm((s, r), BF), vm((s, r), BF),
        vm((s, r), F32),
        vm((2 * s, 1), F32),
        vm((s, r), BF),
        vm((db, r), F32),
        dma(8 + 3 * nq),
        dma(8), dma(8), dma(8), dma(8), dma(7), dma(7),
        dma(nq), dma(nq), dma(nq), dma(nq),
        dma(nq), dma(nq), dma(nq), dma(nq),
        dma(RING), dma(RING), dma(RING), dma(RING),
        dma(RING), dma(RING), dma(RING), dma(RING),
        dma(Z), dma(Z), dma(n_y), dma(n_y),
        dma(1), dma(Z), dma(n_y), dma(n_y),
        dma(3), dma(3), dma(7), dma(7),
        dma(2 * nq + 2),
    ]
    fwd, bwd, grad_down, grad_up = pl.pallas_call(
        functools.partial(kernel, n_pipe),
        out_shape=(
            jax.ShapeDtypeStruct((s, width), BF),
            jax.ShapeDtypeStruct((s, width), BF),
            jax.ShapeDtypeStruct((db, r), F32),
            jax.ShapeDtypeStruct((r, db), F32),
        ),
        in_specs=[
            any_spec, any_spec, any_spec, any_spec, any_spec, vmem_spec, any_spec, any_spec,
            smem_spec, smem_spec, vmem_spec, any_spec, vmem_spec, any_spec, any_spec,
        ],
        out_specs=(any_spec,) * 4,
        scratch_shapes=scratch,
        compiler_params=pltpu.CompilerParams(
            collective_id=0, has_side_effects=True, vmem_limit_bytes=VM * 2**20
        ),
        name="relay",
    )(
        act_in[0, 0], stash_a[0, 0], grad_in[0, 0], text_emb[0], w_vision,
        enc_query[0], enc_key[0], enc_value[0], tok_count, tok_offset,
        merge_gain, w_merge.T, norm_gain.reshape(nq, 1, db), w_down[0], w_up[0],
    )
    return fwd[None, None], bwd[None, None], grad_down[None], grad_up[None]


def solution(mesh):
    in_specs = (
        P("dp", "pipe", None, None),
        P("dp", "pipe", None, None),
        P("dp", "pipe", None, None),
        P("dp", None, "pipe"),
        P("dp", "pipe", None),
        P("dp", "pipe", None),
        P("dp", "pipe", None),
        P("dp", "pipe"),
        P("dp", "pipe"),
        P(),
        P(None, "dp"),
        P(None, "pipe"),
        P("pipe", None),
        P("pipe", "dp", None),
        P("pipe", None, "dp"),
    )
    out_specs = (
        P("dp", "pipe", None, None),
        P("dp", "pipe", None, None),
        P("pipe", "dp", None),
        P("pipe", None, "dp"),
    )
    step = functools.partial(body, mesh.shape["pipe"], mesh.shape["dp"])
    return jax.shard_map(step, mesh=mesh, in_specs=in_specs, out_specs=out_specs, check_vma=False)
```

```python
import functools

import jax
import jax.numpy as jnp
from jax import lax
from jax.experimental import pallas as pl
from jax.experimental.pallas import tpu as pltpu
from jax.sharding import PartitionSpec as P

HEAD_DIM = 128
EPS = 1e-06
RING = 4
Z = 8
VM = 56
TOK = 16
MESH = pl.DeviceIdType.MESH
BF, F32 = jnp.bfloat16, jnp.float32


def mm(a, b):
    return jnp.dot(a, b, preferred_element_type=F32)


def mm_nt(a, b):
    return lax.dot_general(a, b, (((1,), (1,)), ((), ())), preferred_element_type=F32)


def mm_tn(a, b):
    return lax.dot_general(a, b, (((0,), (0,)), ((), ())), preferred_element_type=F32)


def swish(inner):
    return inner * jax.nn.sigmoid(inner)


def pick(k, values):
    out = jnp.int32(values[-1])
    for i in range(len(values) - 2, -1, -1):
        out = jnp.where(k == i, jnp.int32(values[i]), out)
    return out


def rcopy(src, dst, send_sem, recv_sem, device):
    return pltpu.make_async_remote_copy(
        src_ref=src,
        dst_ref=dst,
        send_sem=send_sem,
        recv_sem=recv_sem,
        device_id=device,
        device_id_type=MESH,
    )


FWD = (0, 3, 1, 2)
BWD = (2, 1, 3, 0)
FAR = (3, 4, 5)


def kernel(
    n_pipe,
    act_h, st_h, gin_h, text_h, wv_h, q_ref, ek_h, ev_h, cnt_ref, off_ref, mg_ref, wm_h, gain_ref, wd_h, wu_h,
    fwd_h, bwd_h, gd_h, gu_h,
    X, G, N, wd, wu, xin, O0, B0, nall, but, ups, upr, uxs, uxr, dps, dpr, dxs, dxr, df, accu, accd,
    wm, ek, ev, text, wv, scr, att, tk, fra, frw, rx, ru, rh, rg, rst, rwd, rgn, rb, rp, pk, sc, inner, sig, hid, hidt, bh, bu, bu2, ic, ss, hid2, gdo,
    ld, ags, agr, aus, aur, wms, wmr, zfs, zfr, zbs, zbr, nas, nar, bus, bur,
    ups_s, ups_r, uxs_s, uxs_r, dps_s, dps_r, dxs_s, dxs_r, tzs, tzr, tys, tyr, fzs, fzr, fys, fyr, wzs, wzr, wys, wyr, wxs, wxr, rfs, rfr, rbs, rbr, late, outs,
):
    nq, s2, db = X.shape
    s = s2 // 2
    r = wu.shape[1]
    dp_cols = text.shape[1]
    per = db // dp_cols
    n_y = n_pipe // Z
    width = nq * db
    heads = att.shape[1] // HEAD_DIM

    p, d = lax.axis_index("pipe"), lax.axis_index("dp")
    y, z = p // Z, p % Z
    x, c = d // 2, d % 2
    last = p == n_pipe - 1
    xr, xl, xo = (x + 1) % RING, (x + 3) % RING, (x + 2) % RING

    def at(chip, core):
        return chip * 2 + core

    right, left, other, mate = (p, at(xr, c)), (p, at(xl, c)), (p, at(xo, c)), (p, at(x, 1 - c))

    def cols(ref, q):
        return ref.at[:, pl.ds(pl.multiple_of(q * db, 128), db)]

    def load(i, src, dst):
        return pltpu.make_async_copy(src, dst, ld.at[i])

    small = [
        lambda: load(0, wd_h, wd.at[d]),
        lambda: load(1, wu_h, wu.at[d]),
        lambda: load(2, wm_h, wm.at[d]),
        lambda: load(3, text_h, text),
        lambda: load(4, wv_h, wv),
        lambda: load(5, ek_h, ek),
        lambda: load(6, ev_h, ev),
    ]

    def big(q):
        return (
            load(8 + q, cols(act_h, q), X.at[q, pl.ds(0, s)]),
            load(8 + nq + q, cols(st_h, q), X.at[q, pl.ds(s, s)]),
            load(8 + 2 * nq + q, cols(gin_h, q), G.at[q, pl.ds(s, s)]),
        )

    for copy in small:
        copy().start()

    def start_big(q, carry):
        for copy in big(q):
            copy.start()
        return carry

    lax.fori_loop(0, nq, start_big, 0)

    barrier = pltpu.get_barrier_semaphore()

    def greet(device):
        pl.semaphore_signal(barrier, inc=1, device_id=device, device_id_type=MESH)

    up_wrap = (z == Z - 1) & (y < n_y - 1)
    down_wrap = (z == 0) & (y > 0)
    inside = p < n_pipe - 1
    for i in range(1, nq):
        greet((p, (d + i) % nq))
    for i in range(1, n_y):
        greet((((y + i) % n_y) * Z + z, d))

    @pl.when(inside & jnp.logical_not(up_wrap))
    def _():
        greet((p + 1, d))

    @pl.when(p > 0)
    def _():
        greet((p - 1, d))

    @pl.when(z == 0)
    def _():
        for i in range(2, Z):
            greet((p + i, d))

    expected = nq - 1 + n_y - 1
    for condition in (inside, (p > 0) & jnp.logical_not(down_wrap), z >= 2):
        expected += jnp.where(condition, 1, 0)
    pl.semaphore_wait(barrier, expected)

    @pl.when(up_wrap)
    def _():
        pl.semaphore_signal(late, inc=1, device_id=(p + 1, d), device_id_type=MESH)

    class Gather:
        def __init__(self, buf, send, recv):
            self.buf, self.send, self.recv = buf, send, recv
            self.half = buf.shape[1] // 2

        def copy(self, i):
            lo, hi = pl.ds(0, self.half), pl.ds(self.half, self.half)
            ref, device = (
                lambda: (self.buf.at[d], right),
                lambda: (self.buf.at[d], left),
                lambda: (self.buf.at[at(xl, c), lo], right),
                lambda: (self.buf.at[at(xr, c), hi], left),
                lambda: (self.buf.at[d], mate),
                lambda: (self.buf.at[at(xl, c)], mate),
                lambda: (self.buf.at[at(xr, c)], mate),
                lambda: (self.buf.at[at(xo, c)], mate),
            )[i]()
            return rcopy(ref, ref, self.send.at[i], self.recv.at[i], device)

        def arrival(self, i):
            lo, hi = pl.ds(0, self.half), pl.ds(self.half, self.half)
            ref = (
                lambda: self.buf.at[at(xl, c)],
                lambda: self.buf.at[at(xr, c)],
                lambda: self.buf.at[at(xo, c), lo],
                lambda: self.buf.at[at(xo, c), hi],
                lambda: self.buf.at[at(x, 1 - c)],
                lambda: self.buf.at[at(xl, 1 - c)],
                lambda: self.buf.at[at(xr, 1 - c)],
                lambda: self.buf.at[at(xo, 1 - c)],
            )[i]()
            return rcopy(ref, ref, self.send.at[i], self.recv.at[i], mate)

        def go(self, *which):
            for i in which:
                self.copy(i).start()

        def wait(self, *which):
            for i in which:
                self.arrival(i).wait_recv()

        def drain(self):
            for i in range(8):
                self.copy(i).wait_send()

    down, up = Gather(wd, ags, agr), Gather(wu, aus, aur)

    def merge_copy(i):
        ref, device = (
            lambda: (wm.at[d], right),
            lambda: (wm.at[d], left),
            lambda: (wm.at[d], other),
            lambda: (wm.at[d], mate),
            lambda: (wm.at[at(xl, c)], mate),
            lambda: (wm.at[at(xr, c)], mate),
            lambda: (wm.at[at(xo, c)], mate),
        )[i]()
        return rcopy(ref, ref, wms.at[i], wmr.at[i], device)

    def merge_arrival(i):
        ref = (
            lambda: wm.at[at(xl, c)],
            lambda: wm.at[at(xr, c)],
            lambda: wm.at[at(xo, c)],
            lambda: wm.at[at(x, 1 - c)],
            lambda: wm.at[at(xl, 1 - c)],
            lambda: wm.at[at(xr, 1 - c)],
            lambda: wm.at[at(xo, 1 - c)],
        )[i]()
        return rcopy(ref, ref, wms.at[i], wmr.at[i], mate)

    def to_row(src, dst, send, recv, slot_z):
        return rcopy(src, dst, send.at[0], recv.at[slot_z], (y * Z, d))

    def text_z(slot):
        return to_row(text, fra.at[y, slot], fzs, fzr, slot)

    def map_z(slot):
        return to_row(wv, frw.at[c, y, slot // 2], wzs, wzr, slot)

    def tok_z(slot):
        ref = tk.at[y * Z + slot]
        return to_row(ref, ref, tzs, tzr, slot)

    def to_first(ref, send, recv, slot_y):
        target = jnp.where(y == n_y - 1, 0, y - 1) * Z
        return rcopy(ref, ref, send.at[slot_y], recv.at[slot_y], (target, d))

    def text_y(slot):
        return to_first(fra.at[slot], fys, fyr, slot)

    def map_y(slot):
        return to_first(frw.at[c, slot], wys, wyr, slot)

    def tok_y(slot):
        return to_first(tk.at[pl.ds(slot * Z, Z)], tys, tyr, slot)

    def map_mate(half):
        return rcopy(frw.at[c], frw.at[half], wxs.at[0], wxr.at[0], mate)

    mine = z % 2 == c

    def fwd_send(q):
        return rcopy(O0.at[q], xin.at[q], zfs.at[q], zfr.at[q], (p + 1, d))

    def bwd_send(q):
        return rcopy(B0.at[q], G.at[q, pl.ds(0, s)], zbs.at[q], zbr.at[q], (p - 1, d))

    def raw_f(i):
        src, dst = (
            lambda: (X.at[d, pl.ds(0, s)], rx),
            lambda: (wu.at[d], ru),
            lambda: (hid.at[pl.ds(0, s)], rh),
        )[i]()
        return rcopy(src, dst, rfs.at[i], rfr.at[i], (p + 1, d))

    def raw_b(i):
        src, dst = (
            lambda: (X.at[d, pl.ds(s, s)], rst),
            lambda: (G.at[d, pl.ds(s, s)], rg),
            lambda: (wd.at[d], rwd),
            lambda: (gain_ref.at[d], rgn),
            lambda: (bu, rb.at[pl.ds(0, s)]),
            lambda: (pk, rp),
            lambda: (hid.at[pl.ds(s, s)], rb.at[pl.ds(s, s)]),
        )[i]()
        return rcopy(src, dst, rbs.at[i], rbr.at[i], (p - 1, d))

    def raw_u():
        return rcopy(wu.at[d], rg, rbs.at[1], rbr.at[1], (p - 1, d))

    def fwd_block(j):
        return at((x + pick(j // 2, FWD)) % RING, jnp.where(j % 2 == 0, c, 1 - c))

    def bwd_block(j):
        return at((x + pick(j // 2, BWD)) % RING, jnp.where(j % 2 == 0, 1 - c, c))

    def down_mate(k):
        return rcopy(dps.at[k], dpr.at[k], dps_s.at[k], dps_r.at[k], mate)

    def along_x(src, dst, send, recv, i):
        ref, device = (
            (lambda v: v.at[0, pl.ds(0, r // 2)], left),
            (lambda v: v.at[1], right),
            (lambda v: v.at[2], left),
            (lambda v: v.at[0, pl.ds(r // 2, r // 2)], right),
        )[i]
        return rcopy(ref(src), ref(dst), send.at[i], recv.at[i], device)

    def down_x(i):
        return along_x(dxs, dxr, dxs_s, dxs_r, i)

    def near(src, half, k, total):
        lo, hi = total[:r // 2], total[r // 2:]
        if k == 1:
            hi = hi + half[0, r // 2:].astype(F32)
        else:
            lo = lo + half[0, :r // 2].astype(F32)
        src[k, :r // 2] = lo.astype(BF)
        src[k, r // 2:] = hi.astype(BF)

    def up_mate(k):
        return rcopy(ups.at[k], upr.at[k], ups_s.at[k], ups_r.at[k], mate)

    def up_x(i):
        return along_x(uxs, uxr, uxs_s, uxs_r, i)

    def norm_copy(i):
        target = (d + i) % nq
        return rcopy(N.at[target, pl.ds(0, s)], nall.at[d], nas.at[i], nar.at[i], (p, target))

    def norm_arrival(i):
        ref = nall.at[(d + nq - i) % nq]
        return rcopy(ref, ref, nas.at[i], nar.at[i], mate)

    def but_copy(i):
        return rcopy(but.at[d], but.at[d], bus.at[i], bur.at[i], (p, (d + i) % nq))

    def but_arrival(i):
        ref = but.at[(d + nq - i) % nq]
        return rcopy(ref, ref, bus.at[i], bur.at[i], mate)

    def fwd_out(q):
        return pltpu.make_async_copy(xin.at[q], cols(fwd_h, q), outs.at[q])

    def bwd_out(q):
        return pltpu.make_async_copy(G.at[q, pl.ds(0, s)], cols(bwd_h, q), outs.at[nq + q])

    def each(n, step):
        def run(i, carry):
            step(i)
            return carry

        lax.fori_loop(0, n, run, 0, unroll=True)

    small[0]().wait()
    small[1]().wait()
    down.go(0, 1, 4)
    up.go(0, 1, 4)
    small[2]().wait()
    for i in range(4):
        merge_copy(i).start()

    small[3]().wait()
    small[4]().wait()

    @pl.when(z > 0)
    def _():
        text_z(z).start()

    @pl.when((z > 0) & mine)
    def _():
        map_z(z).start()

    @pl.when(z == 0)
    def _():
        fra[y, 0] = text[...]

    @pl.when((z == 0) & mine)
    def _():
        frw[0, y, 0] = wv[...]

    for copy in big(d):
        copy.wait()

    @pl.when(inside)
    def _():
        raw_f(0).start()
        raw_f(1).start()

    @pl.when((p > 0) & jnp.logical_not(down_wrap))
    def _():
        raw_b(0).start()

    @pl.when((p > 0) & inside & jnp.logical_not(down_wrap))
    def _():
        raw_b(1).start()

    @pl.when(last)
    def _():
        raw_u().start()

    small[5]().wait()
    small[6]().wait()
    query = jnp.concatenate([q_ref[...].astype(F32), jnp.zeros((TOK - q_ref.shape[0], q_ref.shape[1]), F32)], 0)
    query = query.astype(BF)
    for h in range(heads):
        lanes = slice(h * HEAD_DIM, (h + 1) * HEAD_DIM)
        scr[h * TOK:(h + 1) * TOK] = mm_nt(query[:, lanes], ek[:, lanes]) * HEAD_DIM ** (-0.5)
    scores = scr[...]
    weights = jnp.exp(scores - jnp.max(scores, -1, keepdims=True))
    scr[...] = weights / jnp.sum(weights, -1, keepdims=True)
    for h in range(heads):
        lanes = slice(h * HEAD_DIM, (h + 1) * HEAD_DIM)
        att[:, lanes] = mm(scr[h * TOK:(h + 1) * TOK].astype(BF), ev[:, lanes])

    def wait_big(i, carry):
        for copy in big((d + i) % nq):
            copy.wait()
        return carry

    lax.fori_loop(1, nq, wait_big, 0)
    ss[...] = jnp.zeros_like(ss)

    def squares(q):
        v = X[q].astype(F32)
        ss[...] += jnp.sum(v * v, -1, keepdims=True)

    each(nq, squares)
    sc[...] = lax.rsqrt(ss[...] * (1.0 / width) + EPS)

    def normalise(q):
        N[q] = (X[q].astype(F32) * sc[...] * gain_ref[q]).astype(BF)

    each(nq, normalise)

    @pl.when(down_wrap)
    def _():
        pl.semaphore_wait(late, 1)
        raw_b(0).start()
        raw_b(1).start()

    down.wait(0)
    down.go(2, 5)
    down.wait(1)
    down.go(3, 6)
    up.wait(0)
    up.go(2, 5)
    up.wait(1)
    up.go(3, 6)
    for i, k in ((0, 4), (1, 5), (2, 6)):
        merge_arrival(i).wait_recv()
        merge_copy(k).start()
    @pl.when(p > 0)
    def _():
        raw_b(2).start()
        raw_b(3).start()

    @pl.when(z == 0)
    def _():
        for i in range(1, Z):
            text_z(i).wait_recv()

            @pl.when(i % 2 == c)
            def _():
                map_z(i).wait_recv()

        @pl.when(y > 0)
        def _():
            text_y(y).start()
            map_y(y).start()

    order = [fwd_block(j) for j in range(nq)]

    def inner_of(blocks):
        for q in blocks:
            inner[...] += mm(N[q], wd[q])

    def back_of(blocks):
        for q in blocks:
            bh[...] += mm_nt(G[q, s:], wu[q])

    inner[...] = jnp.zeros_like(inner)
    bh[...] = jnp.zeros_like(bh)
    down.wait(4, 5, 6)
    inner_of(order[:6])
    up.wait(4, 5, 6)

    @pl.when(inside)
    def _():
        back_of(order[:6])

    for i in range(3, 7):
        merge_arrival(i).wait_recv()
    rows = att[...].astype(BF).astype(F32)
    scale_m = lax.rsqrt(jnp.mean(rows * rows, -1, keepdims=True) + EPS)
    rows = (rows * scale_m * mg_ref[...][None, :]).astype(BF)
    tokens = mm_nt(rows, wm[...].reshape(nq * wm.shape[1], wm.shape[2]))
    tk[p, :TOK] = jax.nn.gelu(tokens).astype(BF)
    slot = lax.broadcasted_iota(jnp.int32, (TOK, s), 0)
    place = lax.broadcasted_iota(jnp.int32, (TOK, s), 1)
    live = (slot < cnt_ref[0, 0]) & (place == off_ref[0, 0] + slot)
    tk[p, TOK:] = jnp.where(live, 1.0, 0.0).astype(BF)
    @pl.when(z > 0)
    def _():
        tok_z(z).start()

    down.wait(2, 3)
    down.go(7)
    inner_of(order[6:7])
    down.wait(7)
    inner_of(order[7:])
    total = inner[...]
    sig[...] = jax.nn.sigmoid(total)
    hidden = total * sig[...]
    hid[...] = hidden.astype(BF)
    hidt[...] = hidden.T.astype(BF)

    @pl.when(inside)
    def _():
        raw_f(2).start()

    @pl.when(last)
    def _():
        raw_b(6).start()


    def leave(blocks):
        for q in blocks:
            O0[q] = (X[q, :s].astype(F32) + mm(hid[:s], wu[q])).astype(BF)

        @pl.when(inside)
        def _():
            for q in blocks:
                if q is not order[0]:
                    fwd_send(q).start()

        @pl.when(last)
        def _():
            for q in blocks:
                G[q, :s] = O0[q]
                G[q, s:] = (X[q, s:].astype(F32) + mm(hid[s:], wu[q])).astype(BF)
            back_of(blocks)

    leave(order[:4])
    up.wait(2, 3)
    up.go(7)
    for i in range(1, nq):
        if i not in FAR:
            norm_copy(i).start()
    leave(order[4:6])

    @pl.when(inside)
    def _():
        back_of(order[6:7])

    up.wait(7)

    @pl.when(inside)
    def _():
        back_of(order[7:])

    leave(order[6:])
    nall[d] = N[d, :s]

    def factor(rows):
        sg, inn = sig[rows], inner[rows]
        value = (bh[...] * sg * (1.0 + inn * (1.0 - sg))).astype(BF)
        wide = value.astype(F32)
        return value, wide, jnp.sum(wide * inn, -1, keepdims=True) * (1.0 / width)

    hi_rows, lo_rows = slice(s, 2 * s), slice(0, s)

    bu_b, wide_b, mean_b = factor(hi_rows)
    bu[...] = bu_b
    scale_b = sc[hi_rows]
    coef_b = scale_b * mean_b
    columns = jnp.concatenate([jnp.broadcast_to(scale_b, (s, 8)), jnp.broadcast_to(coef_b, (s, s - 8))], 1).T
    pk[...] = columns[4:12]

    @pl.when(p > 0)
    def _():
        raw_b(4).start()
        raw_b(5).start()

    for first in range(0, nq - 1, 4):
        group = [bwd_block(j) for j in range(first, min(first + 4, nq - 1))]
        for q in group:
            back = mm_nt(bu[...], wd[q]) * gain_ref[q]
            value = G[q, s:].astype(F32) + scale_b * (back - X[q, s:].astype(F32) * coef_b)
            B0[q] = value.astype(BF)

        @pl.when(p > 0)
        def _():
            for q in group:
                bwd_send(q).start()

    turned = wide_b.T.astype(BF)
    for k in range(RING):
        dps[k] = mm(turned, N[bwd_block(2 * k), s:]).astype(BF)
    for k in range(RING):
        down_mate(k).start()
    for k in range(RING):
        down_mate(k).wait_recv()
    for k in range(RING):
        value = mm(turned, N[bwd_block(2 * k + 1), s:]) + dpr[k].astype(F32)
        if k == 0:
            dxs[0] = value.astype(BF)
            down_x(0).start()
            down_x(3).start()
        elif k < RING - 1:
            df[k - 1] = value
        else:
            accd[...] = value
    for i in FAR:
        norm_copy(i).start()

    @pl.when(z == 0)
    def _():
        for i in range(1, Z):
            tok_z(i).wait_recv()

        @pl.when(y > 0)
        def _():
            tok_y(y).start()

        for i in range(2, n_y - 1):

            @pl.when((y <= n_y - 1 - i) & (y > 0))
            def _():
                for relay in (text_y, map_y):
                    relay(y + i - 1).wait_recv()
                    relay(y + i - 1).start()

    ss[...] = jnp.zeros_like(ss)
    ic[...] = jnp.zeros_like(ic)
    bh[...] = jnp.zeros_like(bh)

    def take_forward(q):
        v = xin[q].astype(F32)
        ss[:s] += jnp.sum(v * v, -1, keepdims=True)
        ic[...] += mm((v * gain_ref[q]).astype(BF), wd[q])

    def second(j, carry):
        qf, qb = fwd_block(j), jnp.where(j == 0, d, bwd_block(j - 1))

        for i in range(2, n_y - 1):

            @pl.when((z == 0) & (j == 2 * i - 3) & (y <= n_y - 1 - i) & (y > 0))
            def _():
                tok_y(y + i - 1).wait_recv()
                tok_y(y + i - 1).start()

        @pl.when((p > 0) & (j > 0))
        def _():
            fwd_send(qf).wait_recv()

        @pl.when((p > 0) & (j == 0))
        def _():
            for i in range(3):
                raw_f(i).wait_recv()
            xin[d] = (rx[...].astype(F32) + mm(rh[...], ru[...])).astype(BF)

        @pl.when(p > 0)
        def _():
            take_forward(qf)

        @pl.when((j == 4) & (p == 0))
        def _():
            for i in range(1, n_y):
                map_y(i).wait_recv()
            map_mate(c).start()

        @pl.when((j == nq - 2) & (p == 0))
        def _():
            for i in range(1, n_y):
                text_y(i).wait_recv()
                tok_y(i).wait_recv()
            map_mate(1 - c).wait_recv()
            held = tk[:, :TOK].reshape(n_pipe * TOK, r)
            spots = tk[:, TOK:].reshape(n_pipe * TOK, s)
            vision = mm_tn(spots, held).astype(BF)
            marked = mm_tn(spots, jnp.ones_like(held))[:, :1] > 0.5

            def assemble(q):
                for i in range(per):
                    sec = q * per + i
                    mapped = mm(vision, frw[sec % 2, sec // Z, sec % Z // 2])
                    words = fra[sec // Z, sec % Z].astype(F32)
                    xin[q, :, i * dp_cols:(i + 1) * dp_cols] = jnp.where(marked, mapped, words).astype(BF)
                take_forward(q)

            each(nq, assemble)

        @pl.when(j == nq - 1)
        def _():
            scale = lax.rsqrt(ss[:s] * (1.0 / width) + EPS)
            hid2[...] = swish(ic[...] * scale).astype(BF)

            def finish(q):
                xin[q] = (xin[q].astype(F32) + mm(hid2[...], wu[q])).astype(BF)

            each(nq, finish)
            for q in range(nq):
                fwd_out(q).start()

        @pl.when(inside & (j > 0))
        def _():
            bwd_send(qb).wait_recv()

        @pl.when(inside & (j == 0))
        def _():
            for i in range(6):
                raw_b(i).wait_recv()

        @pl.when((p == n_pipe - 2) & (j == 0))
        def _():
            raw_b(6).wait_recv()
            rg[...] = (rst[...].astype(F32) + mm(rb[s:], rg[...])).astype(BF)

        @pl.when(inside & (j == 0))
        def _():
            wide = jnp.concatenate([rp[...], jnp.zeros((s - 8, s), F32)], 0).T
            back = mm_nt(rb[:s], rwd[...]) * rgn[...]
            value = rg[...].astype(F32) + wide[:, 0:1] * (back - rst[...].astype(F32) * wide[:, 4:5])
            G[d, :s] = value.astype(BF)

        bh[...] += mm_nt(G[qb, :s], wu[qb])

        @pl.when(j == nq - 1)
        def _():
            bu_a, wide_a, mean_a = factor(lo_rows)
            but[d] = wide_a.T.astype(BF)
            for i in range(1, nq):
                but_copy(i).start()
            bu2[...] = bu_a
            ss[:s] = mean_a

        term = mm(hidt[...], G[qb])

        @pl.when(j == 0)
        def _():
            accu[...] = term

        @pl.when(j % 2 == 1)
        def _():
            ups[j // 2] = term.astype(BF)
            up_mate(j // 2).start()

        @pl.when(j == 2)
        def _():
            up_mate(0).wait_recv()
            uxs[0] = (term + upr[0].astype(F32)).astype(BF)
            up_x(0).start()
            up_x(3).start()

        for k, part in ((1, 3), (2, 0)):

            @pl.when(j == 2 * k + 2)
            def _():
                up_mate(k).wait_recv()
                up_x(part).wait_recv()
                near(uxs, uxr, k, term + upr[k].astype(F32))
                up_x(k).start()

        @pl.when(j == 1)
        def _():
            for k, part in ((1, 3), (2, 0)):
                down_x(part).wait_recv()
                near(dxs, dxr, k, df[k - 1])
                down_x(k).start()

        return carry

    lax.fori_loop(0, nq, second, 0)

    scale_a = sc[lo_rows]
    coef_a = scale_a * ss[:s]

    def second_backward(q):
        back = mm_nt(bu2[...], wd[q]) * gain_ref[q]
        value = G[q, :s].astype(F32) + scale_a * (back - X[q, :s].astype(F32) * coef_a)
        G[q, :s] = value.astype(BF)

    each(nq, second_backward)
    for q in range(nq):
        bwd_out(q).start()

    for k in (1, 2):
        up_x(k).wait_recv()
    up_mate(RING - 1).wait_recv()
    total = accu[...] + upr[RING - 1].astype(F32)
    for k in (1, 2):
        total += uxr[k].astype(F32)
    accu[...] = total
    up_out = pltpu.make_async_copy(accu, gu_h, outs.at[2 * nq])
    up_out.start()
    for k in (1, 2):
        down_x(k).wait_recv()
    for i in range(1, nq):
        norm_arrival(i).wait_recv()
        but_arrival(i).wait_recv()
    total = accd[...]
    for k in (1, 2):
        total += dxr[k].astype(F32)
    for q in range(nq):
        total += mm(but[q], nall[q])
    gdo[...] = total.T
    down_out = pltpu.make_async_copy(gdo, gd_h, outs.at[2 * nq + 1])
    down_out.start()

    down.drain()
    up.drain()
    for i in range(7):
        merge_copy(i).wait_send()
    @pl.when(z > 0)
    def _():
        text_z(z).wait_send()
        tok_z(z).wait_send()

    @pl.when((z > 0) & mine)
    def _():
        map_z(z).wait_send()

    @pl.when((z == 0) & (y > 0))
    def _():
        for relay in (text_y, map_y, tok_y):
            relay(y).wait_send()
            for i in range(2, n_y - 1):

                @pl.when(y <= n_y - 1 - i)
                def _():
                    relay(y + i - 1).wait_send()

    @pl.when(p == 0)
    def _():
        map_mate(c).wait_send()

    for i in range(1, nq):
        norm_copy(i).wait_send()
        but_copy(i).wait_send()
    for k in range(RING):
        up_mate(k).wait_send()
        down_mate(k).wait_send()
    for i in range(RING):
        up_x(i).wait_send()
        down_x(i).wait_send()

    def drain(q, carry):
        @pl.when(inside & (q != d))
        def _():
            fwd_send(q).wait_send()

        @pl.when((p > 0) & (q != d))
        def _():
            bwd_send(q).wait_send()

        fwd_out(q).wait()
        bwd_out(q).wait()
        return carry

    lax.fori_loop(0, nq, drain, 0)

    @pl.when(inside)
    def _():
        for i in range(3):
            raw_f(i).wait_send()

    @pl.when(p > 0)
    def _():
        for i in range(6):
            raw_b(i).wait_send()

    @pl.when(last)
    def _():
        raw_b(6).wait_send()

    up_out.wait()
    down_out.wait()


PIECES = 4


def hand_over(*refs):
    held, sems = refs[8:12], refs[12]
    loads, stores = [], []
    for i in range(4):
        src, dst = refs[i], refs[4 + i]
        dst = dst.at[0, 0] if len(dst.shape) == 4 else dst.at[0]
        rows = src.shape[0] // PIECES
        for k in range(PIECES):
            part = pl.ds(k * rows, rows)
            n = 2 * (i * PIECES + k)
            loads.append(pltpu.make_async_copy(src.at[part], held[i].at[part], sems.at[n]))
            stores.append(pltpu.make_async_copy(held[i].at[part], dst.at[part], sems.at[n + 1]))
    for copy in loads:
        copy.start()
    for load, store in zip(loads, stores):
        load.wait()
        store.start()
    for copy in stores:
        copy.wait()


def body(
    n_pipe, nq,
    act_in, stash_a, grad_in, text_emb, enc_query, enc_key, enc_value, tok_count, tok_offset,
    merge_gain, w_merge, w_vision, norm_gain, w_down, w_up,
):
    s, width = act_in.shape[2:]
    db, r = w_down.shape[1:]
    enc = enc_query.shape[2]
    heads = enc // HEAD_DIM
    cols = w_vision.shape[1]
    img = enc_key.shape[1]
    n_y = n_pipe // Z
    vm = pltpu.VMEM
    dma = lambda n: pltpu.SemaphoreType.DMA((n,))
    any_spec = pl.BlockSpec(memory_space=pl.ANY)
    hbm_spec = pl.BlockSpec(memory_space=pltpu.HBM)
    vmem_spec = pl.BlockSpec(memory_space=pltpu.VMEM)
    smem_spec = pl.BlockSpec(memory_space=pltpu.SMEM)
    scratch = [
        vm((nq, 2 * s, db), BF),
        vm((nq, 2 * s, db), BF),
        vm((nq, 2 * s, db), BF),
        vm((nq, db, r), BF),
        vm((nq, r, db), BF),
        vm((nq, s, db), BF),
        vm((nq, s, db), BF),
        vm((nq, s, db), BF),
        vm((nq, s, db), BF),
        vm((nq, r, s), BF),
        vm((RING, r, db), BF), vm((RING, r, db), BF), vm((RING, r, db), BF), vm((RING, r, db), BF),
        vm((RING, r, db), BF), vm((RING, r, db), BF), vm((RING, r, db), BF), vm((RING, r, db), BF),
        vm((2, r, db), F32),
        vm((r, db), F32), vm((r, db), F32),
        vm((nq, r // nq, enc), BF),
        vm((img, enc), BF), vm((img, enc), BF),
        vm((s, cols), BF), vm((r, cols), BF),
        vm((heads * TOK, img), F32),
        vm((TOK, enc), F32),
        vm((n_pipe, 2 * TOK, r), BF),
        vm((n_y, Z, s, cols), BF),
        vm((2, n_y, Z // 2, r, cols), BF),
        vm((s, db), BF), vm((r, db), BF), vm((s, r), BF),
        vm((s, db), BF), vm((s, db), BF), vm((db, r), BF), vm((1, db), F32),
        vm((2 * s, r), BF), vm((8, s), F32),
        vm((8, s), F32),
        vm((2 * s, 1), F32),
        vm((2 * s, r), F32), vm((2 * s, r), F32),
        vm((2 * s, r), BF), vm((r, 2 * s), BF),
        vm((s, r), F32), vm((s, r), BF), vm((s, r), BF),
        vm((s, r), F32),
        vm((2 * s, 1), F32),
        vm((s, r), BF),
        vm((db, r), F32),
        dma(8 + 3 * nq),
        dma(8), dma(8), dma(8), dma(8), dma(7), dma(7),
        dma(nq), dma(nq), dma(nq), dma(nq),
        dma(nq), dma(nq), dma(nq), dma(nq),
        dma(RING), dma(RING), dma(RING), dma(RING),
        dma(RING), dma(RING), dma(RING), dma(RING),
        dma(1), dma(Z), dma(n_y), dma(n_y),
        dma(1), dma(Z), dma(n_y), dma(n_y),
        dma(1), dma(Z), dma(n_y), dma(n_y), dma(1), dma(1),
        dma(3), dma(3), dma(7), dma(7),
        pltpu.SemaphoreType.REGULAR,
        dma(2 * nq + 2),
    ]
    fwd, bwd, grad_down, grad_up = pl.pallas_call(
        functools.partial(kernel, n_pipe),
        out_shape=(
            jax.ShapeDtypeStruct((s, width), BF),
            jax.ShapeDtypeStruct((s, width), BF),
            jax.ShapeDtypeStruct((db, r), F32),
            jax.ShapeDtypeStruct((r, db), F32),
        ),
        in_specs=[
            hbm_spec, hbm_spec, hbm_spec, hbm_spec, hbm_spec, vmem_spec, hbm_spec, hbm_spec,
            smem_spec, smem_spec, vmem_spec, hbm_spec, vmem_spec, hbm_spec, hbm_spec,
        ],
        out_specs=(any_spec,) * 4,
        scratch_shapes=scratch,
        compiler_params=pltpu.CompilerParams(
            collective_id=0, has_side_effects=True, vmem_limit_bytes=VM * 2**20
        ),
        name="relay",
    )(
        act_in[0, 0], stash_a[0, 0], grad_in[0, 0], text_emb[0], w_vision,
        enc_query[0], enc_key[0], enc_value[0], tok_count, tok_offset,
        merge_gain, w_merge.T, norm_gain.reshape(nq, 1, db), w_down[0], w_up[0],
    )
    done = pl.pallas_call(
        hand_over,
        out_shape=(
            jax.ShapeDtypeStruct((1, 1, s, width), BF),
            jax.ShapeDtypeStruct((1, 1, s, width), BF),
            jax.ShapeDtypeStruct((1, db, r), F32),
            jax.ShapeDtypeStruct((1, r, db), F32),
        ),
        in_specs=[any_spec] * 4,
        out_specs=(any_spec,) * 4,
        scratch_shapes=[vm((s, width), BF), vm((s, width), BF), vm((db, r), F32), vm((r, db), F32), dma(8 * PIECES)],
        compiler_params=pltpu.CompilerParams(vmem_limit_bytes=VM * 2**20),
        name="hand_over",
    )(fwd, bwd, grad_down, grad_up)
    return done


def solution(mesh):
    in_specs = (
        P("dp", "pipe", None, None),
        P("dp", "pipe", None, None),
        P("dp", "pipe", None, None),
        P("dp", None, "pipe"),
        P("dp", "pipe", None),
        P("dp", "pipe", None),
        P("dp", "pipe", None),
        P("dp", "pipe"),
        P("dp", "pipe"),
        P(),
        P(None, "dp"),
        P(None, "pipe"),
        P("pipe", None),
        P("pipe", "dp", None),
        P("pipe", None, "dp"),
    )
    out_specs = (
        P("dp", "pipe", None, None),
        P("dp", "pipe", None, None),
        P("pipe", "dp", None),
        P("pipe", None, "dp"),
    )
    step = functools.partial(body, mesh.shape["pipe"], mesh.shape["dp"])
    return jax.shard_map(step, mesh=mesh, in_specs=in_specs, out_specs=out_specs, check_vma=False)
```

```python
import functools

import jax
import jax.numpy as jnp
from jax import lax
from jax.experimental import pallas as pl
from jax.experimental.pallas import tpu as pltpu
from jax.sharding import PartitionSpec as P

HEAD_DIM = 128
EPS = 1e-06
RING = 4
Z = 8
VM = 56
TOK = 16
MESH = pl.DeviceIdType.MESH
BF, F32 = jnp.bfloat16, jnp.float32


def mm(a, b):
    return jnp.dot(a, b, preferred_element_type=F32)


def mm_nt(a, b):
    return lax.dot_general(a, b, (((1,), (1,)), ((), ())), preferred_element_type=F32)


def mm_tn(a, b):
    return lax.dot_general(a, b, (((0,), (0,)), ((), ())), preferred_element_type=F32)


def swish(inner):
    return inner * jax.nn.sigmoid(inner)


def pick(k, values):
    out = jnp.int32(values[-1])
    for i in range(len(values) - 2, -1, -1):
        out = jnp.where(k == i, jnp.int32(values[i]), out)
    return out


def rcopy(src, dst, send_sem, recv_sem, device):
    return pltpu.make_async_remote_copy(
        src_ref=src,
        dst_ref=dst,
        send_sem=send_sem,
        recv_sem=recv_sem,
        device_id=device,
        device_id_type=MESH,
    )


FWD = (0, 3, 1, 2)
BWD = (2, 1, 3, 0)
FAR = (3, 4, 5)


def kernel(
    n_pipe,
    act_h, st_h, gin_h, text_h, wv_h, q_ref, ek_h, ev_h, cnt_ref, off_ref, mg_ref, wm_h, gain_ref, wd_h, wu_h,
    fwd_h, bwd_h, gd_h, gu_h,
    X, G, N, wd, wu, xin, O0, B0, nall, but, ups, upr, uxs, uxr, dps, dpr, dxs, dxr, df, accu, accd,
    wm, ek, ev, text, wv, scr, att, tk, fra, frw, rx, ru, rh, rg, rst, rwd, rgn, rb, rp, pk, sc, inner, sig, hid, hidt, bh, bu, bu2, ic, ss, hid2, gdo,
    ld, ags, agr, aus, aur, wms, wmr, zfs, zfr, zbs, zbr, nas, nar, bus, bur,
    ups_s, ups_r, uxs_s, uxs_r, dps_s, dps_r, dxs_s, dxs_r, tzs, tzr, tys, tyr, fzs, fzr, fys, fyr, wzs, wzr, wys, wyr, wxs, wxr, rfs, rfr, rbs, rbr, late, outs,
):
    nq, s2, db = X.shape
    s = s2 // 2
    r = wu.shape[1]
    dp_cols = text.shape[1]
    per = db // dp_cols
    n_y = n_pipe // Z
    width = nq * db
    heads = att.shape[1] // HEAD_DIM

    p, d = lax.axis_index("pipe"), lax.axis_index("dp")
    y, z = p // Z, p % Z
    x, c = d // 2, d % 2
    last = p == n_pipe - 1
    xr, xl, xo = (x + 1) % RING, (x + 3) % RING, (x + 2) % RING

    def at(chip, core):
        return chip * 2 + core

    right, left, other, mate = (p, at(xr, c)), (p, at(xl, c)), (p, at(xo, c)), (p, at(x, 1 - c))

    def cols(ref, q):
        return ref.at[:, pl.ds(pl.multiple_of(q * db, 128), db)]

    def load(i, src, dst):
        return pltpu.make_async_copy(src, dst, ld.at[i])

    small = [
        lambda: load(0, wd_h, wd.at[d]),
        lambda: load(1, wu_h, wu.at[d]),
        lambda: load(2, wm_h, wm.at[d]),
        lambda: load(3, text_h, text),
        lambda: load(4, wv_h, wv),
        lambda: load(5, ek_h, ek),
        lambda: load(6, ev_h, ev),
    ]

    def big(q):
        return (
            load(8 + q, cols(act_h, q), X.at[q, pl.ds(0, s)]),
            load(8 + nq + q, cols(st_h, q), X.at[q, pl.ds(s, s)]),
            load(8 + 2 * nq + q, cols(gin_h, q), G.at[q, pl.ds(s, s)]),
        )

    for copy in small:
        copy().start()

    def start_big(q, carry):
        for copy in big(q):
            copy.start()
        return carry

    lax.fori_loop(0, nq, start_big, 0)

    barrier = pltpu.get_barrier_semaphore()

    def greet(device):
        pl.semaphore_signal(barrier, inc=1, device_id=device, device_id_type=MESH)

    up_wrap = (z == Z - 1) & (y < n_y - 1)
    down_wrap = (z == 0) & (y > 0)
    inside = p < n_pipe - 1
    for i in range(1, nq):
        greet((p, (d + i) % nq))
    for i in range(1, n_y):
        greet((((y + i) % n_y) * Z + z, d))

    @pl.when(inside & jnp.logical_not(up_wrap))
    def _():
        greet((p + 1, d))

    @pl.when(p > 0)
    def _():
        greet((p - 1, d))

    @pl.when(z == 0)
    def _():
        for i in range(2, Z):
            greet((p + i, d))

    expected = nq - 1 + n_y - 1
    for condition in (inside, (p > 0) & jnp.logical_not(down_wrap), z >= 2):
        expected += jnp.where(condition, 1, 0)
    pl.semaphore_wait(barrier, expected)

    @pl.when(up_wrap)
    def _():
        pl.semaphore_signal(late, inc=1, device_id=(p + 1, d), device_id_type=MESH)

    class Gather:
        def __init__(self, buf, send, recv):
            self.buf, self.send, self.recv = buf, send, recv
            self.half = buf.shape[1] // 2

        def copy(self, i):
            lo, hi = pl.ds(0, self.half), pl.ds(self.half, self.half)
            ref, device = (
                lambda: (self.buf.at[d, lo], right),
                lambda: (self.buf.at[d, hi], left),
                lambda: (self.buf.at[at(xl, c), lo], right),
                lambda: (self.buf.at[at(xr, c), hi], left),
                lambda: (self.buf.at[d], mate),
                lambda: (self.buf.at[at(xl, c)], mate),
                lambda: (self.buf.at[at(xr, c)], mate),
                lambda: (self.buf.at[at(xo, c)], mate),
                lambda: (self.buf.at[d, hi], right),
                lambda: (self.buf.at[d, lo], left),
            )[i]()
            return rcopy(ref, ref, self.send.at[i], self.recv.at[i], device)

        def arrival(self, i):
            lo, hi = pl.ds(0, self.half), pl.ds(self.half, self.half)
            ref = (
                lambda: self.buf.at[at(xl, c), lo],
                lambda: self.buf.at[at(xr, c), hi],
                lambda: self.buf.at[at(xo, c), lo],
                lambda: self.buf.at[at(xo, c), hi],
                lambda: self.buf.at[at(x, 1 - c)],
                lambda: self.buf.at[at(xl, 1 - c)],
                lambda: self.buf.at[at(xr, 1 - c)],
                lambda: self.buf.at[at(xo, 1 - c)],
                lambda: self.buf.at[at(xl, c), hi],
                lambda: self.buf.at[at(xr, c), lo],
            )[i]()
            return rcopy(ref, ref, self.send.at[i], self.recv.at[i], mate)

        def go(self, *which):
            for i in which:
                self.copy(i).start()

        def wait(self, *which):
            for i in which:
                self.arrival(i).wait_recv()

        def drain(self):
            for i in range(10):
                self.copy(i).wait_send()

    down, up = Gather(wd, ags, agr), Gather(wu, aus, aur)

    def merge_copy(i):
        ref, device = (
            lambda: (wm.at[d], right),
            lambda: (wm.at[d], left),
            lambda: (wm.at[d], other),
            lambda: (wm.at[d], mate),
            lambda: (wm.at[at(xl, c)], mate),
            lambda: (wm.at[at(xr, c)], mate),
            lambda: (wm.at[at(xo, c)], mate),
        )[i]()
        return rcopy(ref, ref, wms.at[i], wmr.at[i], device)

    def merge_arrival(i):
        ref = (
            lambda: wm.at[at(xl, c)],
            lambda: wm.at[at(xr, c)],
            lambda: wm.at[at(xo, c)],
            lambda: wm.at[at(x, 1 - c)],
            lambda: wm.at[at(xl, 1 - c)],
            lambda: wm.at[at(xr, 1 - c)],
            lambda: wm.at[at(xo, 1 - c)],
        )[i]()
        return rcopy(ref, ref, wms.at[i], wmr.at[i], mate)

    def to_row(src, dst, send, recv, slot_z):
        return rcopy(src, dst, send.at[0], recv.at[slot_z], (y * Z, d))

    def text_z(slot):
        return to_row(text, fra.at[y, slot], fzs, fzr, slot)

    def map_z(slot):
        return to_row(wv, frw.at[c, y, slot // 2], wzs, wzr, slot)

    def tok_z(slot):
        ref = tk.at[y * Z + slot]
        return to_row(ref, ref, tzs, tzr, slot)

    def to_first(ref, send, recv, slot_y):
        target = jnp.where(y == n_y - 1, 0, y - 1) * Z
        return rcopy(ref, ref, send.at[slot_y], recv.at[slot_y], (target, d))

    def text_y(slot):
        return to_first(fra.at[slot], fys, fyr, slot)

    def map_y(slot):
        return to_first(frw.at[c, slot], wys, wyr, slot)

    def tok_y(slot):
        return to_first(tk.at[pl.ds(slot * Z, Z)], tys, tyr, slot)

    def map_mate(half):
        return rcopy(frw.at[c], frw.at[half], wxs.at[0], wxr.at[0], mate)

    mine = z % 2 == c

    def fwd_send(q):
        return rcopy(O0.at[q], xin.at[q], zfs.at[q], zfr.at[q], (p + 1, d))

    def bwd_send(q):
        return rcopy(B0.at[q], G.at[q, pl.ds(0, s)], zbs.at[q], zbr.at[q], (p - 1, d))

    def raw_f(i):
        src, dst = (
            lambda: (X.at[d, pl.ds(0, s)], rx),
            lambda: (wu.at[d], ru),
            lambda: (hid.at[pl.ds(0, s)], rh),
        )[i]()
        return rcopy(src, dst, rfs.at[i], rfr.at[i], (p + 1, d))

    def raw_b(i):
        src, dst = (
            lambda: (X.at[d, pl.ds(s, s)], rst),
            lambda: (G.at[d, pl.ds(s, s)], rg),
            lambda: (wd.at[d], rwd),
            lambda: (gain_ref.at[d], rgn),
            lambda: (bu, rb.at[pl.ds(0, s)]),
            lambda: (pk, rp),
            lambda: (hid.at[pl.ds(s, s)], rb.at[pl.ds(s, s)]),
        )[i]()
        return rcopy(src, dst, rbs.at[i], rbr.at[i], (p - 1, d))

    def raw_u():
        return rcopy(wu.at[d], rg, rbs.at[1], rbr.at[1], (p - 1, d))

    def fwd_block(j):
        return at((x + pick(j // 2, FWD)) % RING, jnp.where(j % 2 == 0, c, 1 - c))

    def bwd_block(j):
        return at((x + pick(j // 2, BWD)) % RING, jnp.where(j % 2 == 0, 1 - c, c))

    def down_mate(k):
        return rcopy(dps.at[k], dpr.at[k], dps_s.at[k], dps_r.at[k], mate)

    def along_x(src, dst, send, recv, i):
        ref, device = (
            (lambda v: v.at[0, pl.ds(0, r // 2)], left),
            (lambda v: v.at[1], right),
            (lambda v: v.at[2], left),
            (lambda v: v.at[0, pl.ds(r // 2, r // 2)], right),
        )[i]
        return rcopy(ref(src), ref(dst), send.at[i], recv.at[i], device)

    def down_x(i):
        return along_x(dxs, dxr, dxs_s, dxs_r, i)

    def near(src, half, k, total):
        lo, hi = total[:r // 2], total[r // 2:]
        if k == 1:
            hi = hi + half[0, r // 2:].astype(F32)
        else:
            lo = lo + half[0, :r // 2].astype(F32)
        src[k, :r // 2] = lo.astype(BF)
        src[k, r // 2:] = hi.astype(BF)

    def up_mate(k):
        return rcopy(ups.at[k], upr.at[k], ups_s.at[k], ups_r.at[k], mate)

    def up_x(i):
        return along_x(uxs, uxr, uxs_s, uxs_r, i)

    def norm_copy(i):
        target = (d + i) % nq
        return rcopy(N.at[target, pl.ds(0, s)], nall.at[d], nas.at[i], nar.at[i], (p, target))

    def norm_arrival(i):
        ref = nall.at[(d + nq - i) % nq]
        return rcopy(ref, ref, nas.at[i], nar.at[i], mate)

    def but_copy(i):
        return rcopy(but.at[d], but.at[d], bus.at[i], bur.at[i], (p, (d + i) % nq))

    def but_arrival(i):
        ref = but.at[(d + nq - i) % nq]
        return rcopy(ref, ref, bus.at[i], bur.at[i], mate)

    def fwd_out(q):
        return pltpu.make_async_copy(xin.at[q], cols(fwd_h, q), outs.at[q])

    def bwd_out(q):
        return pltpu.make_async_copy(G.at[q, pl.ds(0, s)], cols(bwd_h, q), outs.at[nq + q])

    def each(n, step):
        def run(i, carry):
            step(i)
            return carry

        lax.fori_loop(0, n, run, 0, unroll=True)

    small[0]().wait()
    small[1]().wait()
    down.go(0, 1, 8, 9, 4)
    up.go(0, 1, 8, 9, 4)
    small[2]().wait()
    for i in range(4):
        merge_copy(i).start()

    small[3]().wait()
    small[4]().wait()

    @pl.when(z > 0)
    def _():
        text_z(z).start()

    @pl.when((z > 0) & mine)
    def _():
        map_z(z).start()

    @pl.when(z == 0)
    def _():
        fra[y, 0] = text[...]

    @pl.when((z == 0) & mine)
    def _():
        frw[0, y, 0] = wv[...]

    for copy in big(d):
        copy.wait()

    @pl.when(inside)
    def _():
        raw_f(0).start()
        raw_f(1).start()

    @pl.when((p > 0) & jnp.logical_not(down_wrap))
    def _():
        raw_b(0).start()

    @pl.when((p > 0) & inside & jnp.logical_not(down_wrap))
    def _():
        raw_b(1).start()

    @pl.when(last)
    def _():
        raw_u().start()

    small[5]().wait()
    small[6]().wait()
    query = jnp.concatenate([q_ref[...].astype(F32), jnp.zeros((TOK - q_ref.shape[0], q_ref.shape[1]), F32)], 0)
    query = query.astype(BF)
    for h in range(heads):
        lanes = slice(h * HEAD_DIM, (h + 1) * HEAD_DIM)
        scr[h * TOK:(h + 1) * TOK] = mm_nt(query[:, lanes], ek[:, lanes]) * HEAD_DIM ** (-0.5)
    scores = scr[...]
    weights = jnp.exp(scores - jnp.max(scores, -1, keepdims=True))
    scr[...] = weights / jnp.sum(weights, -1, keepdims=True)
    for h in range(heads):
        lanes = slice(h * HEAD_DIM, (h + 1) * HEAD_DIM)
        att[:, lanes] = mm(scr[h * TOK:(h + 1) * TOK].astype(BF), ev[:, lanes])

    def wait_big(i, carry):
        for copy in big((d + i) % nq):
            copy.wait()
        return carry

    lax.fori_loop(1, nq, wait_big, 0)
    ss[...] = jnp.zeros_like(ss)

    def squares(q):
        v = X[q].astype(F32)
        ss[...] += jnp.sum(v * v, -1, keepdims=True)

    each(nq, squares)
    sc[...] = lax.rsqrt(ss[...] * (1.0 / width) + EPS)

    def normalise(q):
        N[q] = (X[q].astype(F32) * sc[...] * gain_ref[q]).astype(BF)

    each(nq, normalise)

    @pl.when(down_wrap)
    def _():
        pl.semaphore_wait(late, 1)
        raw_b(0).start()
        raw_b(1).start()

    for weights in (down, up):
        for i in (0, 1):
            weights.wait(i)
            weights.go(2 + i)
    for weights in (down, up):
        for i in (0, 1):
            weights.wait(8 + i)
            weights.go(5 + i)
    for i, k in ((0, 4), (1, 5), (2, 6)):
        merge_arrival(i).wait_recv()
        merge_copy(k).start()
    @pl.when(p > 0)
    def _():
        raw_b(2).start()
        raw_b(3).start()

    @pl.when(z == 0)
    def _():
        for i in range(1, Z):
            text_z(i).wait_recv()

            @pl.when(i % 2 == c)
            def _():
                map_z(i).wait_recv()

        @pl.when(y > 0)
        def _():
            text_y(y).start()
            map_y(y).start()

    order = [fwd_block(j) for j in range(nq)]

    def inner_of(blocks):
        for q in blocks:
            inner[...] += mm(N[q], wd[q])

    def back_of(blocks):
        for q in blocks:
            bh[...] += mm_nt(G[q, s:], wu[q])

    inner[...] = jnp.zeros_like(inner)
    bh[...] = jnp.zeros_like(bh)
    down.wait(4, 5, 6)
    inner_of(order[:6])
    up.wait(4, 5, 6)

    @pl.when(inside)
    def _():
        back_of(order[:6])

    for i in range(3, 7):
        merge_arrival(i).wait_recv()
    rows = att[...].astype(BF).astype(F32)
    scale_m = lax.rsqrt(jnp.mean(rows * rows, -1, keepdims=True) + EPS)
    rows = (rows * scale_m * mg_ref[...][None, :]).astype(BF)
    tokens = mm_nt(rows, wm[...].reshape(nq * wm.shape[1], wm.shape[2]))
    tk[p, :TOK] = jax.nn.gelu(tokens).astype(BF)
    slot = lax.broadcasted_iota(jnp.int32, (TOK, s), 0)
    place = lax.broadcasted_iota(jnp.int32, (TOK, s), 1)
    live = (slot < cnt_ref[0, 0]) & (place == off_ref[0, 0] + slot)
    tk[p, TOK:] = jnp.where(live, 1.0, 0.0).astype(BF)
    @pl.when(z > 0)
    def _():
        tok_z(z).start()

    down.wait(2, 3)
    down.go(7)
    inner_of(order[6:7])
    down.wait(7)
    inner_of(order[7:])
    total = inner[...]
    sig[...] = jax.nn.sigmoid(total)
    hidden = total * sig[...]
    hid[...] = hidden.astype(BF)
    hidt[...] = hidden.T.astype(BF)

    @pl.when(inside)
    def _():
        raw_f(2).start()

    @pl.when(last)
    def _():
        raw_b(6).start()


    def leave(blocks):
        for q in blocks:
            O0[q] = (X[q, :s].astype(F32) + mm(hid[:s], wu[q])).astype(BF)

        @pl.when(inside)
        def _():
            for q in blocks:
                if q is not order[0]:
                    fwd_send(q).start()

        @pl.when(last)
        def _():
            for q in blocks:
                G[q, :s] = O0[q]

    def own_gradient(blocks):
        @pl.when(last)
        def _():
            for q in blocks:
                G[q, s:] = (X[q, s:].astype(F32) + mm(hid[s:], wu[q])).astype(BF)
            back_of(blocks)

    leave(order[:4])
    own_gradient(order[:4])
    up.wait(2, 3)
    up.go(7)
    for i in range(1, nq):
        if i not in FAR:
            norm_copy(i).start()
    leave(order[4:6])
    own_gradient(order[4:6])

    @pl.when(inside)
    def _():
        back_of(order[6:7])

    up.wait(7)

    @pl.when(inside)
    def _():
        back_of(order[7:])

    own_gradient(order[6:])

    def factor(rows):
        sg, inn = sig[rows], inner[rows]
        value = (bh[...] * sg * (1.0 + inn * (1.0 - sg))).astype(BF)
        wide = value.astype(F32)
        return value, wide, jnp.sum(wide * inn, -1, keepdims=True) * (1.0 / width)

    hi_rows, lo_rows = slice(s, 2 * s), slice(0, s)

    bu_b, wide_b, mean_b = factor(hi_rows)
    bu[...] = bu_b
    scale_b = sc[hi_rows]
    coef_b = scale_b * mean_b
    columns = jnp.concatenate([jnp.broadcast_to(scale_b, (s, 8)), jnp.broadcast_to(coef_b, (s, s - 8))], 1).T
    pk[...] = columns[4:12]

    @pl.when(p > 0)
    def _():
        raw_b(4).start()
        raw_b(5).start()

    for first, stop in ((0, 2), (2, nq - 1)):
        group = [bwd_block(j) for j in range(first, stop)]
        for q in group:
            back = mm_nt(bu[...], wd[q]) * gain_ref[q]
            value = G[q, s:].astype(F32) + scale_b * (back - X[q, s:].astype(F32) * coef_b)
            B0[q] = value.astype(BF)

        @pl.when(p > 0)
        def _():
            for q in group:
                bwd_send(q).start()

        if first == 0:
            leave(order[6:])

    nall[d] = N[d, :s]

    turned = wide_b.T.astype(BF)
    for k in range(RING):
        dps[k] = mm(turned, N[bwd_block(2 * k), s:]).astype(BF)
    for k in range(RING):
        down_mate(k).start()
    for k in range(RING):
        down_mate(k).wait_recv()
    for k in range(RING):
        value = mm(turned, N[bwd_block(2 * k + 1), s:]) + dpr[k].astype(F32)
        if k == 0:
            dxs[0] = value.astype(BF)
            down_x(0).start()
            down_x(3).start()
        elif k < RING - 1:
            df[k - 1] = value
        else:
            accd[...] = value
    for i in FAR:
        norm_copy(i).start()

    @pl.when(z == 0)
    def _():
        for i in range(1, Z):
            tok_z(i).wait_recv()

        @pl.when(y > 0)
        def _():
            tok_y(y).start()

        for i in range(2, n_y - 1):

            @pl.when((y <= n_y - 1 - i) & (y > 0))
            def _():
                for relay in (text_y, map_y):
                    relay(y + i - 1).wait_recv()
                    relay(y + i - 1).start()

    ss[...] = jnp.zeros_like(ss)
    ic[...] = jnp.zeros_like(ic)
    bh[...] = jnp.zeros_like(bh)

    def take_forward(q):
        v = xin[q].astype(F32)
        ss[:s] += jnp.sum(v * v, -1, keepdims=True)
        ic[...] += mm((v * gain_ref[q]).astype(BF), wd[q])

    def forward_output():
        scale = lax.rsqrt(ss[:s] * (1.0 / width) + EPS)
        hid2[...] = swish(ic[...] * scale).astype(BF)

        def finish(q):
            xin[q] = (xin[q].astype(F32) + mm(hid2[...], wu[q])).astype(BF)

        each(nq, finish)
        for q in range(nq):
            fwd_out(q).start()

    def early_sends_done():
        down.drain()
        up.drain()
        for i in range(7):
            merge_copy(i).wait_send()

        @pl.when(z > 0)
        def _():
            text_z(z).wait_send()
            tok_z(z).wait_send()

        @pl.when((z > 0) & mine)
        def _():
            map_z(z).wait_send()

        @pl.when(inside)
        def _():
            for i in range(3):
                raw_f(i).wait_send()

        @pl.when(p > 0)
        def _():
            for i in range(6):
                raw_b(i).wait_send()

        @pl.when(last)
        def _():
            raw_b(6).wait_send()

    def in_turn(j):
        return (p > 0) & ((j < nq - 1) | jnp.logical_not(down_wrap))

    def second(j, carry):
        qf, qb = fwd_block(j), jnp.where(j == 0, d, bwd_block(j - 1))

        for i in range(2, n_y - 1):

            @pl.when((z == 0) & (j == 2 * i - 3) & (y <= n_y - 1 - i) & (y > 0))
            def _():
                tok_y(y + i - 1).wait_recv()
                tok_y(y + i - 1).start()

        @pl.when(in_turn(j) & (j > 0))
        def _():
            fwd_send(qf).wait_recv()

        @pl.when((p > 0) & (j == 0))
        def _():
            for i in range(3):
                raw_f(i).wait_recv()
            xin[d] = (rx[...].astype(F32) + mm(rh[...], ru[...])).astype(BF)

        @pl.when(in_turn(j))
        def _():
            take_forward(qf)

        @pl.when(j == 6)
        def _():
            early_sends_done()

        @pl.when((j == 4) & (p == 0))
        def _():
            for i in range(1, n_y):
                map_y(i).wait_recv()
            map_mate(c).start()

        @pl.when((j == nq - 2) & (p == 0))
        def _():
            for i in range(1, n_y):
                text_y(i).wait_recv()
                tok_y(i).wait_recv()
            map_mate(1 - c).wait_recv()
            held = tk[:, :TOK].reshape(n_pipe * TOK, r)
            spots = tk[:, TOK:].reshape(n_pipe * TOK, s)
            vision = mm_tn(spots, held).astype(BF)
            marked = mm_tn(spots, jnp.ones_like(held))[:, :1] > 0.5

            def assemble(q):
                for i in range(per):
                    sec = q * per + i
                    mapped = mm(vision, frw[sec % 2, sec // Z, sec % Z // 2])
                    words = fra[sec // Z, sec % Z].astype(F32)
                    xin[q, :, i * dp_cols:(i + 1) * dp_cols] = jnp.where(marked, mapped, words).astype(BF)
                take_forward(q)

            each(nq, assemble)

        @pl.when((j == nq - 1) & jnp.logical_not(down_wrap))
        def _():
            forward_output()

        @pl.when(inside & (j > 0))
        def _():
            bwd_send(qb).wait_recv()

        @pl.when(inside & (j == 0))
        def _():
            for i in range(6):
                raw_b(i).wait_recv()

        @pl.when((p == n_pipe - 2) & (j == 0))
        def _():
            raw_b(6).wait_recv()
            rg[...] = (rst[...].astype(F32) + mm(rb[s:], rg[...])).astype(BF)

        @pl.when(inside & (j == 0))
        def _():
            wide = jnp.concatenate([rp[...], jnp.zeros((s - 8, s), F32)], 0).T
            back = mm_nt(rb[:s], rwd[...]) * rgn[...]
            value = rg[...].astype(F32) + wide[:, 0:1] * (back - rst[...].astype(F32) * wide[:, 4:5])
            G[d, :s] = value.astype(BF)

        bh[...] += mm_nt(G[qb, :s], wu[qb])

        @pl.when(j == nq - 1)
        def _():
            bu_a, wide_a, mean_a = factor(lo_rows)
            but[d] = wide_a.T.astype(BF)
            for i in range(1, nq):
                but_copy(i).start()
            bu2[...] = bu_a
            ss[s:] = mean_a

        term = mm(hidt[...], G[qb])

        @pl.when(j == 0)
        def _():
            accu[...] = term

        @pl.when(j % 2 == 1)
        def _():
            ups[j // 2] = term.astype(BF)
            up_mate(j // 2).start()

        @pl.when(j == 2)
        def _():
            up_mate(0).wait_recv()
            uxs[0] = (term + upr[0].astype(F32)).astype(BF)
            up_x(0).start()
            up_x(3).start()

        for k, part in ((1, 3), (2, 0)):

            @pl.when(j == 2 * k + 2)
            def _():
                up_mate(k).wait_recv()
                up_x(part).wait_recv()
                near(uxs, uxr, k, term + upr[k].astype(F32))
                up_x(k).start()

        @pl.when(j == 1)
        def _():
            for k, part in ((1, 3), (2, 0)):
                down_x(part).wait_recv()
                near(dxs, dxr, k, df[k - 1])
                down_x(k).start()

        return carry

    lax.fori_loop(0, nq, second, 0)

    scale_a = sc[lo_rows]
    coef_a = scale_a * ss[s:]

    def second_backward(q):
        back = mm_nt(bu2[...], wd[q]) * gain_ref[q]
        value = G[q, :s].astype(F32) + scale_a * (back - X[q, :s].astype(F32) * coef_a)
        G[q, :s] = value.astype(BF)

    each(nq, second_backward)
    for q in range(nq):
        bwd_out(q).start()

    @pl.when(down_wrap)
    def _():
        q = fwd_block(nq - 1)
        fwd_send(q).wait_recv()
        take_forward(q)
        forward_output()

    for k in (1, 2):
        up_x(k).wait_recv()
    up_mate(RING - 1).wait_recv()
    total = accu[...] + upr[RING - 1].astype(F32)
    for k in (1, 2):
        total += uxr[k].astype(F32)
    accu[...] = total
    up_out = pltpu.make_async_copy(accu, gu_h, outs.at[2 * nq])
    up_out.start()
    for k in (1, 2):
        down_x(k).wait_recv()
    total = accd[...] + mm(but[d], nall[d])
    for k in (1, 2):
        total += dxr[k].astype(F32)
    for i in sorted(range(1, nq), key=lambda i: abs(i - nq // 2), reverse=True):
        norm_arrival(i).wait_recv()
        but_arrival(i).wait_recv()
        q = (d + nq - i) % nq
        total += mm(but[q], nall[q])
    gdo[...] = total.T
    down_out = pltpu.make_async_copy(gdo, gd_h, outs.at[2 * nq + 1])
    down_out.start()

    @pl.when((z == 0) & (y > 0))
    def _():
        for relay in (text_y, map_y, tok_y):
            relay(y).wait_send()
            for i in range(2, n_y - 1):

                @pl.when(y <= n_y - 1 - i)
                def _():
                    relay(y + i - 1).wait_send()

    @pl.when(p == 0)
    def _():
        map_mate(c).wait_send()

    for i in range(1, nq):
        norm_copy(i).wait_send()
        but_copy(i).wait_send()
    for k in range(RING):
        up_mate(k).wait_send()
        down_mate(k).wait_send()
    for i in range(RING):
        up_x(i).wait_send()
        down_x(i).wait_send()

    def drain(q, carry):
        @pl.when(inside & (q != d))
        def _():
            fwd_send(q).wait_send()

        @pl.when((p > 0) & (q != d))
        def _():
            bwd_send(q).wait_send()

        fwd_out(q).wait()
        bwd_out(q).wait()
        return carry

    lax.fori_loop(0, nq, drain, 0)

    up_out.wait()
    down_out.wait()


PIECES = 4


def hand_over(*refs):
    held, sems = refs[8:12], refs[12]
    loads, stores = [], []
    for i in range(4):
        src, dst = refs[i], refs[4 + i]
        dst = dst.at[0, 0] if len(dst.shape) == 4 else dst.at[0]
        rows = src.shape[0] // PIECES
        for k in range(PIECES):
            part = pl.ds(k * rows, rows)
            n = 2 * (i * PIECES + k)
            loads.append(pltpu.make_async_copy(src.at[part], held[i].at[part], sems.at[n]))
            stores.append(pltpu.make_async_copy(held[i].at[part], dst.at[part], sems.at[n + 1]))
    for copy in loads:
        copy.start()
    for load, store in zip(loads, stores):
        load.wait()
        store.start()
    for copy in stores:
        copy.wait()


def body(
    n_pipe, nq,
    act_in, stash_a, grad_in, text_emb, enc_query, enc_key, enc_value, tok_count, tok_offset,
    merge_gain, w_merge, w_vision, norm_gain, w_down, w_up,
):
    s, width = act_in.shape[2:]
    db, r = w_down.shape[1:]
    enc = enc_query.shape[2]
    heads = enc // HEAD_DIM
    cols = w_vision.shape[1]
    img = enc_key.shape[1]
    n_y = n_pipe // Z
    vm = pltpu.VMEM
    dma = lambda n: pltpu.SemaphoreType.DMA((n,))
    any_spec = pl.BlockSpec(memory_space=pl.ANY)
    hbm_spec = pl.BlockSpec(memory_space=pltpu.HBM)
    vmem_spec = pl.BlockSpec(memory_space=pltpu.VMEM)
    smem_spec = pl.BlockSpec(memory_space=pltpu.SMEM)
    scratch = [
        vm((nq, 2 * s, db), BF),
        vm((nq, 2 * s, db), BF),
        vm((nq, 2 * s, db), BF),
        vm((nq, db, r), BF),
        vm((nq, r, db), BF),
        vm((nq, s, db), BF),
        vm((nq, s, db), BF),
        vm((nq, s, db), BF),
        vm((nq, s, db), BF),
        vm((nq, r, s), BF),
        vm((RING, r, db), BF), vm((RING, r, db), BF), vm((RING, r, db), BF), vm((RING, r, db), BF),
        vm((RING, r, db), BF), vm((RING, r, db), BF), vm((RING, r, db), BF), vm((RING, r, db), BF),
        vm((2, r, db), F32),
        vm((r, db), F32), vm((r, db), F32),
        vm((nq, r // nq, enc), BF),
        vm((img, enc), BF), vm((img, enc), BF),
        vm((s, cols), BF), vm((r, cols), BF),
        vm((heads * TOK, img), F32),
        vm((TOK, enc), F32),
        vm((n_pipe, 2 * TOK, r), BF),
        vm((n_y, Z, s, cols), BF),
        vm((2, n_y, Z // 2, r, cols), BF),
        vm((s, db), BF), vm((r, db), BF), vm((s, r), BF),
        vm((s, db), BF), vm((s, db), BF), vm((db, r), BF), vm((1, db), F32),
        vm((2 * s, r), BF), vm((8, s), F32),
        vm((8, s), F32),
        vm((2 * s, 1), F32),
        vm((2 * s, r), F32), vm((2 * s, r), F32),
        vm((2 * s, r), BF), vm((r, 2 * s), BF),
        vm((s, r), F32), vm((s, r), BF), vm((s, r), BF),
        vm((s, r), F32),
        vm((2 * s, 1), F32),
        vm((s, r), BF),
        vm((db, r), F32),
        dma(8 + 3 * nq),
        dma(10), dma(10), dma(10), dma(10), dma(7), dma(7),
        dma(nq), dma(nq), dma(nq), dma(nq),
        dma(nq), dma(nq), dma(nq), dma(nq),
        dma(RING), dma(RING), dma(RING), dma(RING),
        dma(RING), dma(RING), dma(RING), dma(RING),
        dma(1), dma(Z), dma(n_y), dma(n_y),
        dma(1), dma(Z), dma(n_y), dma(n_y),
        dma(1), dma(Z), dma(n_y), dma(n_y), dma(1), dma(1),
        dma(3), dma(3), dma(7), dma(7),
        pltpu.SemaphoreType.REGULAR,
        dma(2 * nq + 2),
    ]
    fwd, bwd, grad_down, grad_up = pl.pallas_call(
        functools.partial(kernel, n_pipe),
        out_shape=(
            jax.ShapeDtypeStruct((s, width), BF),
            jax.ShapeDtypeStruct((s, width), BF),
            jax.ShapeDtypeStruct((db, r), F32),
            jax.ShapeDtypeStruct((r, db), F32),
        ),
        in_specs=[
            hbm_spec, hbm_spec, hbm_spec, hbm_spec, hbm_spec, vmem_spec, hbm_spec, hbm_spec,
            smem_spec, smem_spec, vmem_spec, hbm_spec, vmem_spec, hbm_spec, hbm_spec,
        ],
        out_specs=(any_spec,) * 4,
        scratch_shapes=scratch,
        compiler_params=pltpu.CompilerParams(
            collective_id=0, has_side_effects=True, vmem_limit_bytes=VM * 2**20
        ),
        name="relay",
    )(
        act_in[0, 0], stash_a[0, 0], grad_in[0, 0], text_emb[0], w_vision,
        enc_query[0], enc_key[0], enc_value[0], tok_count, tok_offset,
        merge_gain, w_merge.T, norm_gain.reshape(nq, 1, db), w_down[0], w_up[0],
    )
    done = pl.pallas_call(
        hand_over,
        out_shape=(
            jax.ShapeDtypeStruct((1, 1, s, width), BF),
            jax.ShapeDtypeStruct((1, 1, s, width), BF),
            jax.ShapeDtypeStruct((1, db, r), F32),
            jax.ShapeDtypeStruct((1, r, db), F32),
        ),
        in_specs=[any_spec] * 4,
        out_specs=(any_spec,) * 4,
        scratch_shapes=[vm((s, width), BF), vm((s, width), BF), vm((db, r), F32), vm((r, db), F32), dma(8 * PIECES)],
        compiler_params=pltpu.CompilerParams(vmem_limit_bytes=VM * 2**20),
        name="hand_over",
    )(fwd, bwd, grad_down, grad_up)
    return done


def solution(mesh):
    in_specs = (
        P("dp", "pipe", None, None),
        P("dp", "pipe", None, None),
        P("dp", "pipe", None, None),
        P("dp", None, "pipe"),
        P("dp", "pipe", None),
        P("dp", "pipe", None),
        P("dp", "pipe", None),
        P("dp", "pipe"),
        P("dp", "pipe"),
        P(),
        P(None, "dp"),
        P(None, "pipe"),
        P("pipe", None),
        P("pipe", "dp", None),
        P("pipe", None, "dp"),
    )
    out_specs = (
        P("dp", "pipe", None, None),
        P("dp", "pipe", None, None),
        P("pipe", "dp", None),
        P("pipe", None, "dp"),
    )
    step = functools.partial(body, mesh.shape["pipe"], mesh.shape["dp"])
    return jax.shard_map(step, mesh=mesh, in_specs=in_specs, out_specs=out_specs, check_vma=False)
```

```python
import functools

import jax
import jax.numpy as jnp
from jax import lax
from jax.experimental import pallas as pl
from jax.experimental.pallas import tpu as pltpu
from jax.sharding import PartitionSpec as P

HEAD_DIM = 128
EPS = 1e-06
RING = 4
Z = 8
VM = 56
TOK = 16
MESH = pl.DeviceIdType.MESH
BF, F32 = jnp.bfloat16, jnp.float32


def mm(a, b):
    return jnp.dot(a, b, preferred_element_type=F32)


def mm_nt(a, b):
    return lax.dot_general(a, b, (((1,), (1,)), ((), ())), preferred_element_type=F32)


def mm_tn(a, b):
    return lax.dot_general(a, b, (((0,), (0,)), ((), ())), preferred_element_type=F32)


def swish(inner):
    return inner * jax.nn.sigmoid(inner)


def pick(k, values):
    out = jnp.int32(values[-1])
    for i in range(len(values) - 2, -1, -1):
        out = jnp.where(k == i, jnp.int32(values[i]), out)
    return out


def rcopy(src, dst, send_sem, recv_sem, device):
    return pltpu.make_async_remote_copy(
        src_ref=src,
        dst_ref=dst,
        send_sem=send_sem,
        recv_sem=recv_sem,
        device_id=device,
        device_id_type=MESH,
    )


FWD = (0, 3, 1, 2)
BWD = (2, 1, 3, 0)
FAR = (3, 4, 5)


def kernel(
    n_pipe,
    act_h, st_h, gin_h, text_h, wv_h, q_ref, ek_h, ev_h, cnt_ref, off_ref, mg_ref, wm_h, gain_ref, wd_h, wu_h,
    fwd_h, bwd_h, gd_h, gu_h,
    X, G, N, wd, wu, xin, O0, B0, nall, but, ups, upr, uxs, uxr, dps, dpr, dxs, dxr, df, accu, accd,
    wm, ek, ev, text, wv, scr, att, tk, fra, frw, rx, ru, rh, rg, rst, rwd, rgn, rb, rp, pk, sc, inner, sig, hid, hidt, bh, bu, bu2, ic, ss, hid2, gdo,
    ld, ags, agr, aus, aur, wms, wmr, zfs, zfr, zbs, zbr, nas, nar, bus, bur,
    ups_s, ups_r, uxs_s, uxs_r, dps_s, dps_r, dxs_s, dxs_r, tzs, tzr, tys, tyr, fzs, fzr, fys, fyr, wzs, wzr, wys, wyr, wxs, wxr, rfs, rfr, rbs, rbr, late, outs,
):
    nq, s2, db = X.shape
    s = s2 // 2
    r = wu.shape[1]
    dp_cols = text.shape[1]
    per = db // dp_cols
    n_y = n_pipe // Z
    width = nq * db
    heads = att.shape[1] // HEAD_DIM

    p, d = lax.axis_index("pipe"), lax.axis_index("dp")
    y, z = p // Z, p % Z
    x, c = d // 2, d % 2
    last = p == n_pipe - 1
    xr, xl, xo = (x + 1) % RING, (x + 3) % RING, (x + 2) % RING

    def at(chip, core):
        return chip * 2 + core

    right, left, other, mate = (p, at(xr, c)), (p, at(xl, c)), (p, at(xo, c)), (p, at(x, 1 - c))

    def cols(ref, q):
        return ref.at[:, pl.ds(pl.multiple_of(q * db, 128), db)]

    def load(i, src, dst):
        return pltpu.make_async_copy(src, dst, ld.at[i])

    small = [
        lambda: load(0, wd_h, wd.at[d]),
        lambda: load(1, wu_h, wu.at[d]),
        lambda: load(2, wm_h, wm.at[d]),
        lambda: load(3, text_h, text),
        lambda: load(4, wv_h, wv),
        lambda: load(5, ek_h, ek),
        lambda: load(6, ev_h, ev),
    ]

    def big(q):
        return (
            load(8 + q, cols(act_h, q), X.at[q, pl.ds(0, s)]),
            load(8 + nq + q, cols(st_h, q), X.at[q, pl.ds(s, s)]),
            load(8 + 2 * nq + q, cols(gin_h, q), G.at[q, pl.ds(s, s)]),
        )

    for copy in small:
        copy().start()

    def start_big(q, carry):
        for copy in big(q):
            copy.start()
        return carry

    lax.fori_loop(0, nq, start_big, 0)

    barrier = pltpu.get_barrier_semaphore()

    def greet(device):
        pl.semaphore_signal(barrier, inc=1, device_id=device, device_id_type=MESH)

    up_wrap = (z == Z - 1) & (y < n_y - 1)
    down_wrap = (z == 0) & (y > 0)
    inside = p < n_pipe - 1
    for i in range(1, nq):
        greet((p, (d + i) % nq))
    for i in range(1, n_y):
        greet((((y + i) % n_y) * Z + z, d))

    @pl.when(inside & jnp.logical_not(up_wrap))
    def _():
        greet((p + 1, d))

    @pl.when(p > 0)
    def _():
        greet((p - 1, d))

    @pl.when(z == 0)
    def _():
        for i in range(2, Z):
            greet((p + i, d))

    expected = nq - 1 + n_y - 1
    for condition in (inside, (p > 0) & jnp.logical_not(down_wrap), z >= 2):
        expected += jnp.where(condition, 1, 0)
    pl.semaphore_wait(barrier, expected)

    @pl.when(up_wrap)
    def _():
        pl.semaphore_signal(late, inc=1, device_id=(p + 1, d), device_id_type=MESH)

    class Gather:
        def __init__(self, buf, send, recv):
            self.buf, self.send, self.recv = buf, send, recv
            self.half = buf.shape[1] // 2

        def copy(self, i):
            lo, hi = pl.ds(0, self.half), pl.ds(self.half, self.half)
            ref, device = (
                lambda: (self.buf.at[d, lo], right),
                lambda: (self.buf.at[d, hi], left),
                lambda: (self.buf.at[at(xl, c), lo], right),
                lambda: (self.buf.at[at(xr, c), hi], left),
                lambda: (self.buf.at[d], mate),
                lambda: (self.buf.at[at(xl, c)], mate),
                lambda: (self.buf.at[at(xr, c)], mate),
                lambda: (self.buf.at[at(xo, c)], mate),
                lambda: (self.buf.at[d, hi], right),
                lambda: (self.buf.at[d, lo], left),
            )[i]()
            return rcopy(ref, ref, self.send.at[i], self.recv.at[i], device)

        def arrival(self, i):
            lo, hi = pl.ds(0, self.half), pl.ds(self.half, self.half)
            ref = (
                lambda: self.buf.at[at(xl, c), lo],
                lambda: self.buf.at[at(xr, c), hi],
                lambda: self.buf.at[at(xo, c), lo],
                lambda: self.buf.at[at(xo, c), hi],
                lambda: self.buf.at[at(x, 1 - c)],
                lambda: self.buf.at[at(xl, 1 - c)],
                lambda: self.buf.at[at(xr, 1 - c)],
                lambda: self.buf.at[at(xo, 1 - c)],
                lambda: self.buf.at[at(xl, c), hi],
                lambda: self.buf.at[at(xr, c), lo],
            )[i]()
            return rcopy(ref, ref, self.send.at[i], self.recv.at[i], mate)

        def go(self, *which):
            for i in which:
                self.copy(i).start()

        def wait(self, *which):
            for i in which:
                self.arrival(i).wait_recv()

        def drain(self):
            for i in range(10):
                self.copy(i).wait_send()

    down, up = Gather(wd, ags, agr), Gather(wu, aus, aur)

    def merge_copy(i):
        ref, device = (
            lambda: (wm.at[d], right),
            lambda: (wm.at[d], left),
            lambda: (wm.at[d], other),
            lambda: (wm.at[d], mate),
            lambda: (wm.at[at(xl, c)], mate),
            lambda: (wm.at[at(xr, c)], mate),
            lambda: (wm.at[at(xo, c)], mate),
        )[i]()
        return rcopy(ref, ref, wms.at[i], wmr.at[i], device)

    def merge_arrival(i):
        ref = (
            lambda: wm.at[at(xl, c)],
            lambda: wm.at[at(xr, c)],
            lambda: wm.at[at(xo, c)],
            lambda: wm.at[at(x, 1 - c)],
            lambda: wm.at[at(xl, 1 - c)],
            lambda: wm.at[at(xr, 1 - c)],
            lambda: wm.at[at(xo, 1 - c)],
        )[i]()
        return rcopy(ref, ref, wms.at[i], wmr.at[i], mate)

    def to_row(src, dst, send, recv, slot_z):
        return rcopy(src, dst, send.at[0], recv.at[slot_z], (y * Z, d))

    def text_z(slot):
        return to_row(text, fra.at[y, slot], fzs, fzr, slot)

    def map_z(slot):
        return to_row(wv, frw.at[c, y, slot // 2], wzs, wzr, slot)

    def tok_z(slot):
        ref = tk.at[y * Z + slot]
        return to_row(ref, ref, tzs, tzr, slot)

    def to_first(ref, send, recv, slot_y):
        target = jnp.where(y == n_y - 1, 0, jnp.maximum(y - 1, 0)) * Z
        return rcopy(ref, ref, send.at[slot_y], recv.at[slot_y], (target, d))

    def text_y(slot):
        return to_first(fra.at[slot], fys, fyr, slot)

    def map_y(slot):
        return to_first(frw.at[c, slot], wys, wyr, slot)

    def tok_y(slot):
        return to_first(tk.at[pl.ds(slot * Z, Z)], tys, tyr, slot)

    def map_mate(half):
        return rcopy(frw.at[c], frw.at[half], wxs.at[0], wxr.at[0], mate)

    mine = z % 2 == c

    ahead, behind = ((p + 1) % n_pipe, d), ((p + n_pipe - 1) % n_pipe, d)

    def fwd_send(q):
        return rcopy(O0.at[q], xin.at[q], zfs.at[q], zfr.at[q], ahead)

    def bwd_send(q):
        return rcopy(B0.at[q], G.at[q, pl.ds(0, s)], zbs.at[q], zbr.at[q], behind)

    def raw_f(i):
        src, dst = (
            lambda: (X.at[d, pl.ds(0, s)], rx),
            lambda: (wu.at[d], ru),
            lambda: (hid.at[pl.ds(0, s)], rh),
        )[i]()
        return rcopy(src, dst, rfs.at[i], rfr.at[i], ahead)

    def raw_b(i):
        src, dst = (
            lambda: (X.at[d, pl.ds(s, s)], rst),
            lambda: (G.at[d, pl.ds(s, s)], rg),
            lambda: (wd.at[d], rwd),
            lambda: (gain_ref.at[d], rgn),
            lambda: (bu, rb.at[pl.ds(0, s)]),
            lambda: (pk, rp),
            lambda: (hid.at[pl.ds(s, s)], rb.at[pl.ds(s, s)]),
        )[i]()
        return rcopy(src, dst, rbs.at[i], rbr.at[i], behind)

    def raw_u():
        return rcopy(wu.at[d], rg, rbs.at[1], rbr.at[1], behind)

    def fwd_block(j):
        return at((x + pick(j // 2, FWD)) % RING, jnp.where(j % 2 == 0, c, 1 - c))

    def bwd_block(j):
        return at((x + pick(j // 2, BWD)) % RING, jnp.where(j % 2 == 0, 1 - c, c))

    def down_mate(k):
        return rcopy(dps.at[k], dpr.at[k], dps_s.at[k], dps_r.at[k], mate)

    def along_x(src, dst, send, recv, i):
        ref, device = (
            (lambda v: v.at[0, pl.ds(0, r // 2)], left),
            (lambda v: v.at[1], right),
            (lambda v: v.at[2], left),
            (lambda v: v.at[0, pl.ds(r // 2, r // 2)], right),
        )[i]
        return rcopy(ref(src), ref(dst), send.at[i], recv.at[i], device)

    def down_x(i):
        return along_x(dxs, dxr, dxs_s, dxs_r, i)

    def near(src, half, k, total):
        lo, hi = total[:r // 2], total[r // 2:]
        if k == 1:
            hi = hi + half[0, r // 2:].astype(F32)
        else:
            lo = lo + half[0, :r // 2].astype(F32)
        src[k, :r // 2] = lo.astype(BF)
        src[k, r // 2:] = hi.astype(BF)

    def up_mate(k):
        return rcopy(ups.at[k], upr.at[k], ups_s.at[k], ups_r.at[k], mate)

    def up_x(i):
        return along_x(uxs, uxr, uxs_s, uxs_r, i)

    def norm_copy(i):
        target = (d + i) % nq
        return rcopy(N.at[target, pl.ds(0, s)], nall.at[d], nas.at[i], nar.at[i], (p, target))

    def norm_arrival(i):
        ref = nall.at[(d + nq - i) % nq]
        return rcopy(ref, ref, nas.at[i], nar.at[i], mate)

    def but_copy(i):
        return rcopy(but.at[d], but.at[d], bus.at[i], bur.at[i], (p, (d + i) % nq))

    def but_arrival(i):
        ref = but.at[(d + nq - i) % nq]
        return rcopy(ref, ref, bus.at[i], bur.at[i], mate)

    def fwd_out(q):
        return pltpu.make_async_copy(xin.at[q], cols(fwd_h, q), outs.at[q])

    def bwd_out(q):
        return pltpu.make_async_copy(G.at[q, pl.ds(0, s)], cols(bwd_h, q), outs.at[nq + q])

    def each(n, step):
        def run(i, carry):
            step(i)
            return carry

        lax.fori_loop(0, n, run, 0, unroll=True)

    small[0]().wait()
    small[1]().wait()
    down.go(0, 1, 8, 9, 4)
    up.go(0, 1, 8, 9, 4)
    small[2]().wait()
    for i in range(4):
        merge_copy(i).start()

    small[3]().wait()
    small[4]().wait()

    @pl.when(z > 0)
    def _():
        text_z(z).start()

    @pl.when((z > 0) & mine)
    def _():
        map_z(z).start()

    @pl.when(z == 0)
    def _():
        fra[y, 0] = text[...]

    @pl.when((z == 0) & mine)
    def _():
        frw[0, y, 0] = wv[...]

    for copy in big(d):
        copy.wait()

    @pl.when(inside)
    def _():
        raw_f(0).start()
        raw_f(1).start()

    @pl.when((p > 0) & jnp.logical_not(down_wrap))
    def _():
        raw_b(0).start()

    @pl.when((p > 0) & inside & jnp.logical_not(down_wrap))
    def _():
        raw_b(1).start()

    @pl.when(last)
    def _():
        raw_u().start()

    small[5]().wait()
    small[6]().wait()
    query = jnp.concatenate([q_ref[...].astype(F32), jnp.zeros((TOK - q_ref.shape[0], q_ref.shape[1]), F32)], 0)
    query = query.astype(BF)
    for h in range(heads):
        lanes = slice(h * HEAD_DIM, (h + 1) * HEAD_DIM)
        scr[h * TOK:(h + 1) * TOK] = mm_nt(query[:, lanes], ek[:, lanes]) * HEAD_DIM ** (-0.5)
    scores = scr[...]
    weights = jnp.exp(scores - jnp.max(scores, -1, keepdims=True))
    scr[...] = weights / jnp.sum(weights, -1, keepdims=True)
    for h in range(heads):
        lanes = slice(h * HEAD_DIM, (h + 1) * HEAD_DIM)
        att[:, lanes] = mm(scr[h * TOK:(h + 1) * TOK].astype(BF), ev[:, lanes])

    def wait_big(i, carry):
        for copy in big((d + i) % nq):
            copy.wait()
        return carry

    lax.fori_loop(1, nq, wait_big, 0)
    ss[...] = jnp.zeros_like(ss)

    def squares(q):
        v = X[q].astype(F32)
        ss[...] += jnp.sum(v * v, -1, keepdims=True)

    each(nq, squares)
    sc[...] = lax.rsqrt(ss[...] * (1.0 / width) + EPS)

    def normalise(q):
        N[q] = (X[q].astype(F32) * sc[...] * gain_ref[q]).astype(BF)

    each(nq, normalise)

    @pl.when(down_wrap)
    def _():
        pl.semaphore_wait(late, 1)
        raw_b(0).start()
        raw_b(1).start()

    for weights in (down, up):
        for i in (0, 1):
            weights.wait(i)
            weights.go(2 + i)
    for weights in (down, up):
        for i in (0, 1):
            weights.wait(8 + i)
            weights.go(5 + i)
    for i, k in ((0, 4), (1, 5), (2, 6)):
        merge_arrival(i).wait_recv()
        merge_copy(k).start()
    @pl.when(p > 0)
    def _():
        raw_b(2).start()
        raw_b(3).start()

    @pl.when(z == 0)
    def _():
        for i in range(1, Z):
            text_z(i).wait_recv()

            @pl.when(i % 2 == c)
            def _():
                map_z(i).wait_recv()

        @pl.when(y > 0)
        def _():
            text_y(y).start()
            map_y(y).start()

    order = [fwd_block(j) for j in range(nq)]

    def inner_of(blocks):
        for q in blocks:
            inner[...] += mm(N[q], wd[q])

    def back_of(blocks):
        for q in blocks:
            bh[...] += mm_nt(G[q, s:], wu[q])

    inner[...] = jnp.zeros_like(inner)
    bh[...] = jnp.zeros_like(bh)
    down.wait(4, 5, 6)
    inner_of(order[:6])
    up.wait(4, 5, 6)

    @pl.when(inside)
    def _():
        back_of(order[:6])

    for i in range(3, 7):
        merge_arrival(i).wait_recv()
    rows = att[...].astype(BF).astype(F32)
    scale_m = lax.rsqrt(jnp.mean(rows * rows, -1, keepdims=True) + EPS)
    rows = (rows * scale_m * mg_ref[...][None, :]).astype(BF)
    tokens = mm_nt(rows, wm[...].reshape(nq * wm.shape[1], wm.shape[2]))
    tk[p, :TOK] = jax.nn.gelu(tokens).astype(BF)
    slot = lax.broadcasted_iota(jnp.int32, (TOK, s), 0)
    place = lax.broadcasted_iota(jnp.int32, (TOK, s), 1)
    live = (slot < cnt_ref[0, 0]) & (place == off_ref[0, 0] + slot)
    tk[p, TOK:] = jnp.where(live, 1.0, 0.0).astype(BF)
    @pl.when(z > 0)
    def _():
        tok_z(z).start()

    down.wait(2, 3)
    down.go(7)
    inner_of(order[6:7])
    down.wait(7)
    inner_of(order[7:])
    total = inner[...]
    sig[...] = jax.nn.sigmoid(total)
    hidden = total * sig[...]
    hid[...] = hidden.astype(BF)
    hidt[...] = hidden.T.astype(BF)

    @pl.when(inside)
    def _():
        raw_f(2).start()

    @pl.when(last)
    def _():
        raw_b(6).start()


    def leave(blocks):
        for q in blocks:
            O0[q] = (X[q, :s].astype(F32) + mm(hid[:s], wu[q])).astype(BF)

        @pl.when(inside)
        def _():
            for q in blocks:
                if q is not order[0]:
                    fwd_send(q).start()

        @pl.when(last)
        def _():
            for q in blocks:
                G[q, :s] = O0[q]

    def own_gradient(blocks):
        @pl.when(last)
        def _():
            for q in blocks:
                G[q, s:] = (X[q, s:].astype(F32) + mm(hid[s:], wu[q])).astype(BF)
            back_of(blocks)

    leave(order[:4])
    own_gradient(order[:4])
    up.wait(2, 3)
    up.go(7)
    for i in range(1, nq):
        if i not in FAR:
            norm_copy(i).start()
    leave(order[4:6])
    own_gradient(order[4:6])

    @pl.when(inside)
    def _():
        back_of(order[6:7])

    up.wait(7)

    @pl.when(inside)
    def _():
        back_of(order[7:])

    own_gradient(order[6:])

    def factor(rows):
        sg, inn = sig[rows], inner[rows]
        value = (bh[...] * sg * (1.0 + inn * (1.0 - sg))).astype(BF)
        wide = value.astype(F32)
        return value, wide, jnp.sum(wide * inn, -1, keepdims=True) * (1.0 / width)

    hi_rows, lo_rows = slice(s, 2 * s), slice(0, s)

    bu_b, wide_b, mean_b = factor(hi_rows)
    bu[...] = bu_b
    scale_b = sc[hi_rows]
    coef_b = scale_b * mean_b
    columns = jnp.concatenate([jnp.broadcast_to(scale_b, (s, 8)), jnp.broadcast_to(coef_b, (s, s - 8))], 1).T
    pk[...] = columns[4:12]

    @pl.when(p > 0)
    def _():
        raw_b(4).start()
        raw_b(5).start()

    for first, stop in ((0, 2), (2, nq - 1)):
        group = [bwd_block(j) for j in range(first, stop)]
        for q in group:
            back = mm_nt(bu[...], wd[q]) * gain_ref[q]
            value = G[q, s:].astype(F32) + scale_b * (back - X[q, s:].astype(F32) * coef_b)
            B0[q] = value.astype(BF)

        @pl.when(p > 0)
        def _():
            for q in group:
                bwd_send(q).start()

        if first == 0:
            leave(order[6:])

    nall[d] = N[d, :s]

    turned = wide_b.T.astype(BF)
    for k in range(RING):
        dps[k] = mm(turned, N[bwd_block(2 * k), s:]).astype(BF)
    for k in range(RING):
        down_mate(k).start()
    for k in range(RING):
        down_mate(k).wait_recv()
    for k in range(RING):
        value = mm(turned, N[bwd_block(2 * k + 1), s:]) + dpr[k].astype(F32)
        if k == 0:
            dxs[0] = value.astype(BF)
            down_x(0).start()
            down_x(3).start()
        elif k < RING - 1:
            df[k - 1] = value
        else:
            accd[...] = value
    for i in FAR:
        norm_copy(i).start()

    @pl.when(z == 0)
    def _():
        for i in range(1, Z):
            tok_z(i).wait_recv()

        @pl.when(y > 0)
        def _():
            tok_y(y).start()

        for i in range(2, n_y - 1):

            @pl.when((y <= n_y - 1 - i) & (y > 0))
            def _():
                for relay in (text_y, map_y):
                    relay(y + i - 1).wait_recv()
                    relay(y + i - 1).start()

    ss[...] = jnp.zeros_like(ss)
    ic[...] = jnp.zeros_like(ic)
    bh[...] = jnp.zeros_like(bh)

    def take_forward(q):
        v = xin[q].astype(F32)
        ss[:s] += jnp.sum(v * v, -1, keepdims=True)
        ic[...] += mm((v * gain_ref[q]).astype(BF), wd[q])

    def forward_output():
        scale = lax.rsqrt(ss[:s] * (1.0 / width) + EPS)
        hid2[...] = swish(ic[...] * scale).astype(BF)

        def finish(q):
            xin[q] = (xin[q].astype(F32) + mm(hid2[...], wu[q])).astype(BF)

        each(nq, finish)
        for q in range(nq):
            fwd_out(q).start()

    def early_sends_done():
        down.drain()
        up.drain()
        for i in range(7):
            merge_copy(i).wait_send()

        @pl.when(z > 0)
        def _():
            text_z(z).wait_send()
            tok_z(z).wait_send()

        @pl.when((z > 0) & mine)
        def _():
            map_z(z).wait_send()

        @pl.when(inside)
        def _():
            for i in range(3):
                raw_f(i).wait_send()

        @pl.when(p > 0)
        def _():
            for i in range(6):
                raw_b(i).wait_send()

        @pl.when(last)
        def _():
            raw_b(6).wait_send()

    def in_turn(j):
        return (p > 0) & ((j < nq - 1) | jnp.logical_not(down_wrap))

    def second(j, carry):
        qf, qb = fwd_block(j), jnp.where(j == 0, d, bwd_block(j - 1))

        for i in range(2, n_y - 1):

            @pl.when((z == 0) & (j == 2 * i - 3) & (y <= n_y - 1 - i) & (y > 0))
            def _():
                tok_y(y + i - 1).wait_recv()
                tok_y(y + i - 1).start()

        @pl.when(in_turn(j) & (j > 0))
        def _():
            fwd_send(qf).wait_recv()

        @pl.when((p > 0) & (j == 0))
        def _():
            for i in range(3):
                raw_f(i).wait_recv()
            xin[d] = (rx[...].astype(F32) + mm(rh[...], ru[...])).astype(BF)

        @pl.when(in_turn(j))
        def _():
            take_forward(qf)

        @pl.when(j == 6)
        def _():
            early_sends_done()

        @pl.when((j == 4) & (p == 0))
        def _():
            for i in range(1, n_y):
                map_y(i).wait_recv()
            map_mate(c).start()

        @pl.when((j == nq - 2) & (p == 0))
        def _():
            for i in range(1, n_y):
                text_y(i).wait_recv()
                tok_y(i).wait_recv()
            map_mate(1 - c).wait_recv()
            held = tk[:, :TOK].reshape(n_pipe * TOK, r)
            spots = tk[:, TOK:].reshape(n_pipe * TOK, s)
            vision = mm_tn(spots, held).astype(BF)
            marked = mm_tn(spots, jnp.ones_like(held))[:, :1] > 0.5

            def assemble(q):
                for i in range(per):
                    sec = q * per + i
                    mapped = mm(vision, frw[sec % 2, sec // Z, sec % Z // 2])
                    words = fra[sec // Z, sec % Z].astype(F32)
                    xin[q, :, i * dp_cols:(i + 1) * dp_cols] = jnp.where(marked, mapped, words).astype(BF)
                take_forward(q)

            each(nq, assemble)

        @pl.when((j == nq - 1) & jnp.logical_not(down_wrap))
        def _():
            forward_output()

        @pl.when(inside & (j > 0))
        def _():
            bwd_send(qb).wait_recv()

        @pl.when(inside & (j == 0))
        def _():
            for i in range(6):
                raw_b(i).wait_recv()

        @pl.when((p == n_pipe - 2) & (j == 0))
        def _():
            raw_b(6).wait_recv()
            rg[...] = (rst[...].astype(F32) + mm(rb[s:], rg[...])).astype(BF)

        @pl.when(inside & (j == 0))
        def _():
            wide = jnp.concatenate([rp[...], jnp.zeros((s - 8, s), F32)], 0).T
            back = mm_nt(rb[:s], rwd[...]) * rgn[...]
            value = rg[...].astype(F32) + wide[:, 0:1] * (back - rst[...].astype(F32) * wide[:, 4:5])
            G[d, :s] = value.astype(BF)

        bh[...] += mm_nt(G[qb, :s], wu[qb])

        @pl.when(j == nq - 1)
        def _():
            bu_a, wide_a, mean_a = factor(lo_rows)
            but[d] = wide_a.T.astype(BF)
            for i in range(1, nq):
                but_copy(i).start()
            bu2[...] = bu_a
            ss[s:] = mean_a

        term = mm(hidt[...], G[qb])

        @pl.when(j == 0)
        def _():
            accu[...] = term

        @pl.when(j % 2 == 1)
        def _():
            ups[j // 2] = term.astype(BF)
            up_mate(j // 2).start()

        @pl.when(j == 2)
        def _():
            up_mate(0).wait_recv()
            uxs[0] = (term + upr[0].astype(F32)).astype(BF)
            up_x(0).start()
            up_x(3).start()

        for k, part in ((1, 3), (2, 0)):

            @pl.when(j == 2 * k + 2)
            def _():
                up_mate(k).wait_recv()
                up_x(part).wait_recv()
                near(uxs, uxr, k, term + upr[k].astype(F32))
                up_x(k).start()

        @pl.when(j == 1)
        def _():
            for k, part in ((1, 3), (2, 0)):
                down_x(part).wait_recv()
                near(dxs, dxr, k, df[k - 1])
                down_x(k).start()

        return carry

    lax.fori_loop(0, nq, second, 0)

    scale_a = sc[lo_rows]
    coef_a = scale_a * ss[s:]

    def second_backward(q):
        back = mm_nt(bu2[...], wd[q]) * gain_ref[q]
        value = G[q, :s].astype(F32) + scale_a * (back - X[q, :s].astype(F32) * coef_a)
        G[q, :s] = value.astype(BF)

    each(nq, second_backward)
    for q in range(nq):
        bwd_out(q).start()

    @pl.when(down_wrap)
    def _():
        q = fwd_block(nq - 1)
        fwd_send(q).wait_recv()
        take_forward(q)
        forward_output()

    for k in (1, 2):
        up_x(k).wait_recv()
    up_mate(RING - 1).wait_recv()
    total = accu[...] + upr[RING - 1].astype(F32)
    for k in (1, 2):
        total += uxr[k].astype(F32)
    accu[...] = total
    up_out = pltpu.make_async_copy(accu, gu_h, outs.at[2 * nq])
    up_out.start()
    for k in (1, 2):
        down_x(k).wait_recv()
    total = accd[...] + mm(but[d], nall[d])
    for k in (1, 2):
        total += dxr[k].astype(F32)
    for i in sorted(range(1, nq), key=lambda i: abs(i - nq // 2), reverse=True):
        norm_arrival(i).wait_recv()
        but_arrival(i).wait_recv()
        q = (d + nq - i) % nq
        total += mm(but[q], nall[q])
    gdo[...] = total.T
    down_out = pltpu.make_async_copy(gdo, gd_h, outs.at[2 * nq + 1])
    down_out.start()

    @pl.when((z == 0) & (y > 0))
    def _():
        for relay in (text_y, map_y, tok_y):
            relay(y).wait_send()
            for i in range(2, n_y - 1):

                @pl.when(y <= n_y - 1 - i)
                def _():
                    relay(y + i - 1).wait_send()

    @pl.when(p == 0)
    def _():
        map_mate(c).wait_send()

    for i in range(1, nq):
        norm_copy(i).wait_send()
        but_copy(i).wait_send()
    for k in range(RING):
        up_mate(k).wait_send()
        down_mate(k).wait_send()
    for i in range(RING):
        up_x(i).wait_send()
        down_x(i).wait_send()

    def drain(q, carry):
        @pl.when(inside & (q != d))
        def _():
            fwd_send(q).wait_send()

        @pl.when((p > 0) & (q != d))
        def _():
            bwd_send(q).wait_send()

        fwd_out(q).wait()
        bwd_out(q).wait()
        return carry

    lax.fori_loop(0, nq, drain, 0)

    up_out.wait()
    down_out.wait()


PIECES = 4


def hand_over(*refs):
    held, sems = refs[8:12], refs[12]
    loads, stores = [], []
    for i in range(4):
        src, dst = refs[i], refs[4 + i]
        dst = dst.at[0, 0] if len(dst.shape) == 4 else dst.at[0]
        rows = src.shape[0] // PIECES
        for k in range(PIECES):
            part = pl.ds(k * rows, rows)
            n = 2 * (i * PIECES + k)
            loads.append(pltpu.make_async_copy(src.at[part], held[i].at[part], sems.at[n]))
            stores.append(pltpu.make_async_copy(held[i].at[part], dst.at[part], sems.at[n + 1]))
    for copy in loads:
        copy.start()
    for load, store in zip(loads, stores):
        load.wait()
        store.start()
    for copy in stores:
        copy.wait()


def body(
    n_pipe, nq,
    act_in, stash_a, grad_in, text_emb, enc_query, enc_key, enc_value, tok_count, tok_offset,
    merge_gain, w_merge, w_vision, norm_gain, w_down, w_up,
):
    s, width = act_in.shape[2:]
    db, r = w_down.shape[1:]
    enc = enc_query.shape[2]
    heads = enc // HEAD_DIM
    cols = w_vision.shape[1]
    img = enc_key.shape[1]
    n_y = n_pipe // Z
    vm = pltpu.VMEM
    dma = lambda n: pltpu.SemaphoreType.DMA((n,))
    any_spec = pl.BlockSpec(memory_space=pl.ANY)
    hbm_spec = pl.BlockSpec(memory_space=pltpu.HBM)
    vmem_spec = pl.BlockSpec(memory_space=pltpu.VMEM)
    smem_spec = pl.BlockSpec(memory_space=pltpu.SMEM)
    scratch = [
        vm((nq, 2 * s, db), BF),
        vm((nq, 2 * s, db), BF),
        vm((nq, 2 * s, db), BF),
        vm((nq, db, r), BF),
        vm((nq, r, db), BF),
        vm((nq, s, db), BF),
        vm((nq, s, db), BF),
        vm((nq, s, db), BF),
        vm((nq, s, db), BF),
        vm((nq, r, s), BF),
        vm((RING, r, db), BF), vm((RING, r, db), BF), vm((RING, r, db), BF), vm((RING, r, db), BF),
        vm((RING, r, db), BF), vm((RING, r, db), BF), vm((RING, r, db), BF), vm((RING, r, db), BF),
        vm((2, r, db), F32),
        vm((r, db), F32), vm((r, db), F32),
        vm((nq, r // nq, enc), BF),
        vm((img, enc), BF), vm((img, enc), BF),
        vm((s, cols), BF), vm((r, cols), BF),
        vm((heads * TOK, img), F32),
        vm((TOK, enc), F32),
        vm((n_pipe, 2 * TOK, r), BF),
        vm((n_y, Z, s, cols), BF),
        vm((2, n_y, Z // 2, r, cols), BF),
        vm((s, db), BF), vm((r, db), BF), vm((s, r), BF),
        vm((s, db), BF), vm((s, db), BF), vm((db, r), BF), vm((1, db), F32),
        vm((2 * s, r), BF), vm((8, s), F32),
        vm((8, s), F32),
        vm((2 * s, 1), F32),
        vm((2 * s, r), F32), vm((2 * s, r), F32),
        vm((2 * s, r), BF), vm((r, 2 * s), BF),
        vm((s, r), F32), vm((s, r), BF), vm((s, r), BF),
        vm((s, r), F32),
        vm((2 * s, 1), F32),
        vm((s, r), BF),
        vm((db, r), F32),
        dma(8 + 3 * nq),
        dma(10), dma(10), dma(10), dma(10), dma(7), dma(7),
        dma(nq), dma(nq), dma(nq), dma(nq),
        dma(nq), dma(nq), dma(nq), dma(nq),
        dma(RING), dma(RING), dma(RING), dma(RING),
        dma(RING), dma(RING), dma(RING), dma(RING),
        dma(1), dma(Z), dma(n_y), dma(n_y),
        dma(1), dma(Z), dma(n_y), dma(n_y),
        dma(1), dma(Z), dma(n_y), dma(n_y), dma(1), dma(1),
        dma(3), dma(3), dma(7), dma(7),
        pltpu.SemaphoreType.REGULAR,
        dma(2 * nq + 2),
    ]
    fwd, bwd, grad_down, grad_up = pl.pallas_call(
        functools.partial(kernel, n_pipe),
        out_shape=(
            jax.ShapeDtypeStruct((s, width), BF),
            jax.ShapeDtypeStruct((s, width), BF),
            jax.ShapeDtypeStruct((db, r), F32),
            jax.ShapeDtypeStruct((r, db), F32),
        ),
        in_specs=[
            hbm_spec, hbm_spec, hbm_spec, hbm_spec, hbm_spec, vmem_spec, hbm_spec, hbm_spec,
            smem_spec, smem_spec, vmem_spec, hbm_spec, vmem_spec, hbm_spec, hbm_spec,
        ],
        out_specs=(any_spec,) * 4,
        scratch_shapes=scratch,
        compiler_params=pltpu.CompilerParams(
            collective_id=0, has_side_effects=True, vmem_limit_bytes=VM * 2**20
        ),
        name="relay",
    )(
        act_in[0, 0], stash_a[0, 0], grad_in[0, 0], text_emb[0], w_vision,
        enc_query[0], enc_key[0], enc_value[0], tok_count, tok_offset,
        merge_gain, w_merge.T, norm_gain.reshape(nq, 1, db), w_down[0], w_up[0],
    )
    done = pl.pallas_call(
        hand_over,
        out_shape=(
            jax.ShapeDtypeStruct((1, 1, s, width), BF),
            jax.ShapeDtypeStruct((1, 1, s, width), BF),
            jax.ShapeDtypeStruct((1, db, r), F32),
            jax.ShapeDtypeStruct((1, r, db), F32),
        ),
        in_specs=[any_spec] * 4,
        out_specs=(any_spec,) * 4,
        scratch_shapes=[vm((s, width), BF), vm((s, width), BF), vm((db, r), F32), vm((r, db), F32), dma(8 * PIECES)],
        compiler_params=pltpu.CompilerParams(vmem_limit_bytes=VM * 2**20),
        name="hand_over",
    )(fwd, bwd, grad_down, grad_up)
    return done


def solution(mesh):
    in_specs = (
        P("dp", "pipe", None, None),
        P("dp", "pipe", None, None),
        P("dp", "pipe", None, None),
        P("dp", None, "pipe"),
        P("dp", "pipe", None),
        P("dp", "pipe", None),
        P("dp", "pipe", None),
        P("dp", "pipe"),
        P("dp", "pipe"),
        P(),
        P(None, "dp"),
        P(None, "pipe"),
        P("pipe", None),
        P("pipe", "dp", None),
        P("pipe", None, "dp"),
    )
    out_specs = (
        P("dp", "pipe", None, None),
        P("dp", "pipe", None, None),
        P("pipe", "dp", None),
        P("pipe", None, "dp"),
    )
    step = functools.partial(body, mesh.shape["pipe"], mesh.shape["dp"])
    return jax.shard_map(step, mesh=mesh, in_specs=in_specs, out_specs=out_specs, check_vma=False)
```
